128 devices in a mesh: req: 4 (over y), tile: 32 (over x, z, core).
Axes of the slice: x: 4, y: 4, z: 4, core: 2. Of those that a mesh axis runs over, the one named last changes fastest.
Arguments:
- latent: bfloat16 [16, 4, 64, 32, 16], P('req', None, 'tile'), may hold values from -6 to 6
- destination: int32 [16, 1], replicated, may hold values from 0 to 3; in each aligned block of 4 rows (0 to 3, 4 to 7, ...) at most 2 rows name the same one
- valid_frames: int32 [16], replicated, may hold values from 1 to 4
- cache_slot: int32 [16], replicated, may hold values from 0 to 15, each once
- latent_cache: bfloat16 [64, 2, 64, 32, 16], P('req', None, 'tile'), may hold values from -6 to 6
- feature_cache: bfloat16 [64, 2, 64, 32, 384], P('req', None, 'tile'), may hold values from -6 to 6
- in_weight: bfloat16 [3, 3, 3, 16, 384], replicated, may hold values from -0.3125 to 0.3125
- in_bias: float32 [384], replicated, may hold values from -4 to 4
- norm_gain: float32 [384], replicated, may hold values from 0.1 to 1.9
- time_weight: bfloat16 [3, 384, 768], replicated, may hold values from -0.1875 to 0.1875
- time_bias: float32 [768], replicated, may hold values from -3 to 3
- out_weight: bfloat16 [3, 3, 384, 192], replicated, may hold values from -0.109375 to 0.109375
- out_bias: float32 [192], replicated, may hold values from -3 to 3
Outputs:
- decoded: bfloat16 [32, 8, 128, 64, 192], P('req', None, 'tile')
The draws below stay inside these ranges and needn't reach their ends.
Inputs may be any that keep to these rules, and one draw needn't show every extreme that they name: `destination`: request r starts on index r // 4 of req. Among the 4 requests of one index no group is named more than 2 times, and in some such block one group is named exactly 2 times. `cache_slot`: each value once.
All inputs are finite; a program needn't handle non-finite values.
Results may differ from the reference program's by a relative error of at most 0.0051.
Values may be sent and summed in bfloat16 or wider, within the bound.
A program may use at most 320 MiB of HBM per device.

```python
import math
import jax
import jax.numpy as jnp
import numpy as np
from jax import lax

LATENT_CHANNELS = 16
MIDDLE_CHANNELS = 384
OUTPUT_CHANNELS = 192
FRAMES = 4
LOCAL_REQUESTS = 4
WIDTH = 32
CAPACITY = 2
REQUESTS = 16
SLOTS = 8
ALL_SLOTS = 32
HEIGHT = 64
N_REQ = 4


def touch_ends(values, rng, least, largest):
    longest = values.shape.index(max(values.shape))
    spots = []
    for shift in (0, 1):
        where = [jax.random.randint(jax.random.fold_in(rng, axis), (), 0, length) for axis, length in enumerate(values.shape)]
        where[longest] = (where[longest] + shift) % values.shape[longest]
        spots.append(tuple(where))
    return values.at[spots[0]].set(least).at[spots[1]].set(largest)


def shard_levels(key, shape, shards, least, high):
    gain, own = 1.0, jax.random.fold_in(key, 6)
    for dim, blocks in shards:
        heights = jnp.exp(jax.random.uniform(jax.random.fold_in(own, dim), (blocks,), jnp.float32, least / len(shards), high / len(shards)))
        gain = gain * jnp.repeat(heights, shape[dim] // blocks).reshape([-1 if axis == dim else 1 for axis in range(len(shape))])
    return gain


def routed_block(rng, own, number, rows, amount, top, limit, lean):
    order = jax.random.permutation(rng, amount)
    heavy_load, ordinary = load_shares(amount, rows * top, limit, lean, True), load_shares(amount, rows * top, limit, lean, False)
    places = jnp.arange(amount)

    def named(tallies, turn):
        used = int((tallies > 0).sum())
        fixed = max(1, used // 4)
        passed = fixed + (places - fixed + turn * (used - fixed)) % max(1, amount - fixed)
        return jnp.zeros((amount,), jnp.int32).at[order[jnp.where(places < fixed, places, passed)]].set(jnp.asarray(tallies, jnp.int32))

    tallies = jnp.where(number % 4 == 0, named(heavy_load, number // 4), named(ordinary, number - number // 4 - 1))
    mixed = jax.random.permutation(jax.random.fold_in(own, 3), amount)
    donor, taker = mixed[0:amount // 2 * 2:2], mixed[1:amount // 2 * 2:2]
    slack = jnp.minimum(tallies[donor] - 1, limit - tallies[taker]) // 2
    slack = jnp.where((donor == order[0]) | (taker == order[0]) | (tallies[taker] == 0), 0, jnp.maximum(slack, 0))
    passed = jax.random.randint(jax.random.fold_in(own, 4), (amount // 2,), 0, 1 << 20) % (slack + 1)
    tallies = tallies.at[donor].add(-passed).at[taker].add(passed)
    items = jnp.searchsorted(jnp.cumsum(tallies), jnp.arange(rows * top), side="right").astype(jnp.int32)
    table = items.reshape(top, rows).T
    table = table[jax.random.permutation(jax.random.fold_in(own, 1), rows)]
    turn = jax.random.randint(jax.random.fold_in(own, 2), (rows, 1), 0, top)
    return jnp.take_along_axis(table, (jnp.arange(top)[None, :] + turn) % top, axis=1)


def load_shares(count, total, reach, skew, full):
    weights = [(1 << 20) // math.isqrt(standing ** skew) + 1 for standing in range(1, count + 1)]
    largest = reach if full else min(reach, max(-(-total // count), total * weights[0] // sum(weights)))
    least = 1 if total - largest >= count - 1 else 0
    counts, spare = [largest] + [least] * (count - 1), total - largest - least * (count - 1)
    while spare > 0:
        movable = [i for i in range(1, count) if counts[i] < largest] or [i for i in range(1, count) if counts[i] < reach]
        whole, budget = sum([weights[i] for i in movable]), spare
        for i in movable:
            addition = min(reach - counts[i], max(1, budget * weights[i] // whole), spare)
            counts[i] = counts[i] + addition
            spare = spare - addition
    return np.array(counts)


def gaussian(stream_key, extent, spread, reach, cuts=(), held_as=jnp.bfloat16):
    values = spread * jax.random.normal(stream_key, extent, jnp.float32)
    if cuts:
        values = values * shard_levels(stream_key, extent, cuts, -0.22, 0.18)
    return jnp.clip(values, -reach, reach).astype(held_as)


def setup_inputs(seed: int = 0) -> dict:
    key_list = jax.random.split(jax.random.key(seed), 14)
    latent = gaussian(key_list[0], (REQUESTS, FRAMES, HEIGHT, WIDTH, LATENT_CHANNELS), 1.0, 6.0, ((0, 4), (2, 32)))
    destination_keys = jax.random.split(jax.random.fold_in(key_list[1], 1), REQUESTS // LOCAL_REQUESTS)
    destination_turns = jax.random.permutation(jax.random.fold_in(key_list[1], 3), REQUESTS // LOCAL_REQUESTS)
    destination = jax.vmap(lambda own, number: routed_block(jax.random.fold_in(key_list[1], 2), own, number, LOCAL_REQUESTS, N_REQ, 1, CAPACITY, 2))(destination_keys, destination_turns).reshape((REQUESTS, 1))
    valid_frames = touch_ends(jax.random.randint(key_list[2], (REQUESTS,), 1, FRAMES + 1), jax.random.fold_in(key_list[2], 1), 1, FRAMES).astype(jnp.int32)
    cache_slot = jax.random.permutation(key_list[3], REQUESTS).astype(jnp.int32)
    latent_cache = gaussian(key_list[4], (N_REQ * REQUESTS, 2, HEIGHT, WIDTH, LATENT_CHANNELS), 1.0, 6.0, ((0, 4), (2, 32)))
    feature_cache = gaussian(key_list[5], (N_REQ * REQUESTS, 2, HEIGHT, WIDTH, MIDDLE_CHANNELS), 1.0, 6.0, ((0, 4), (2, 32)))
    in_weight = gaussian(key_list[6], (3, 3, 3, LATENT_CHANNELS, MIDDLE_CHANNELS), (27 * LATENT_CHANNELS) ** -0.5, 0.3125)
    in_bias = gaussian(key_list[7], (MIDDLE_CHANNELS,), 1.0, 4.0, (), jnp.float32)
    norm_gain = jnp.clip(1.0 + 0.18 * jax.random.normal(key_list[8], (MIDDLE_CHANNELS,), jnp.float32), 0.1, 1.9)
    time_weight = gaussian(key_list[9], (3, MIDDLE_CHANNELS, 2 * MIDDLE_CHANNELS), (3 * MIDDLE_CHANNELS) ** -0.5, 0.1875)
    time_bias = gaussian(key_list[10], (2 * MIDDLE_CHANNELS,), 0.5, 3.0, (), jnp.float32)
    out_weight = gaussian(key_list[11], (3, 3, MIDDLE_CHANNELS, OUTPUT_CHANNELS), (9 * MIDDLE_CHANNELS) ** -0.5, 0.109375)
    out_bias = gaussian(key_list[12], (OUTPUT_CHANNELS,), 0.5, 3.0, (), jnp.float32)
    return dict(latent=latent, destination=destination, valid_frames=valid_frames, cache_slot=cache_slot, latent_cache=latent_cache, feature_cache=feature_cache, in_weight=in_weight, in_bias=in_bias, norm_gain=norm_gain, time_weight=time_weight, time_bias=time_bias, out_weight=out_weight, out_bias=out_bias)


EPSILON = 1e-06

def rank_within(flat_target, per_source):
    positions = jnp.arange(flat_target.shape[0])
    source = positions // per_source
    earlier = (source[:, None] == source[None, :]) & (flat_target[:, None] == flat_target[None, :]) & (positions[None, :] < positions[:, None])
    return (source, lax.optimization_barrier(jnp.sum(earlier.astype(jnp.int32), axis=1)))

def patch_stack(padded, row_count, column_count):
    pieces = []
    for time_step in range(3):
        for row_step in range(3):
            for column_step in range(3):
                pieces.append(padded[..., time_step:time_step + FRAMES, row_step:row_step + row_count, column_step:column_step + column_count, :])
    return jnp.concatenate(pieces, axis=-1)

def normed_silu(inner_sum, norm_gain):
    norm_scale = lax.rsqrt(lax.optimization_barrier(jnp.mean(inner_sum * inner_sum, axis=-1, keepdims=True)) + EPSILON)
    return jax.nn.silu(inner_sum * norm_scale * norm_gain)

def temporal(sequence, time_weight, time_bias):
    running = time_bias
    for time_step in range(3):
        running = running + jnp.dot(sequence[..., time_step:time_step + FRAMES, :, :, :], time_weight[time_step], preferred_element_type=jnp.float32)
    return running

def spatial_conv(padded, out_weight, row_count, column_count):
    running = jnp.zeros(padded.shape[:-3] + (row_count, column_count, out_weight.shape[-1]), jnp.float32)
    for row_step in range(3):
        for column_step in range(3):
            running = running + jnp.dot(padded[..., row_step:row_step + row_count, column_step:column_step + column_count, :], out_weight[row_step, column_step], preferred_element_type=jnp.float32)
    return running

def reference(latent, destination, valid_frames, cache_slot, latent_cache, feature_cache, in_weight, in_bias, norm_gain, time_weight, time_bias, out_weight, out_bias):
    flat_target = destination[:, 0].astype(jnp.int32)
    source, order_rank = rank_within(flat_target, LOCAL_REQUESTS)
    position = (flat_target * SLOTS + source * CAPACITY + order_rank).astype(jnp.int32)
    slot_latent = jnp.zeros((ALL_SLOTS,) + latent.shape[1:], latent.dtype).at[position].set(latent)
    slot_frames = jnp.zeros((ALL_SLOTS,), jnp.int32).at[position].set(valid_frames.astype(jnp.int32))
    slot_row = jnp.zeros((ALL_SLOTS,), jnp.int32).at[position].set((flat_target * REQUESTS + cache_slot).astype(jnp.int32))
    flat_in = in_weight.reshape(27 * LATENT_CHANNELS, MIDDLE_CHANNELS)

    def decode_slot(members):
        arrived_latent, frames_valid, cache_row = members
        kept_frames = jnp.arange(FRAMES) < frames_valid
        masked = jnp.where(kept_frames[:, None, None, None], arrived_latent, jnp.zeros_like(arrived_latent))
        frames = jnp.concatenate([latent_cache[cache_row], masked], axis=0)
        padded = jnp.pad(frames, ((0, 0), (1, 1), (1, 1), (0, 0)))
        stacked = patch_stack(padded, HEIGHT, WIDTH)
        inner_sum = jnp.dot(stacked, flat_in, preferred_element_type=jnp.float32) + in_bias
        active = normed_silu(inner_sum, norm_gain).astype(jnp.bfloat16)
        sequence = jnp.concatenate([feature_cache[cache_row], active], axis=0)
        doubled = temporal(sequence, time_weight, time_bias).astype(jnp.bfloat16)
        halves = jnp.stack([doubled[..., :MIDDLE_CHANNELS], doubled[..., MIDDLE_CHANNELS:]], axis=1)
        upsampled = halves.reshape(2 * FRAMES, HEIGHT, WIDTH, MIDDLE_CHANNELS)
        upsampled = jnp.repeat(jnp.repeat(upsampled, 2, axis=1), 2, axis=2)
        padded_up = jnp.pad(upsampled, ((0, 0), (1, 1), (1, 1), (0, 0)))
        result = spatial_conv(padded_up, out_weight, 2 * HEIGHT, 2 * WIDTH) + out_bias
        shown_frames = jnp.arange(2 * FRAMES) // 2 < frames_valid
        return jnp.where(shown_frames[:, None, None, None], result, 0.0).astype(jnp.bfloat16)
    return lax.map(decode_slot, (slot_latent, slot_frames, slot_row))
```

```python
import functools

import jax
import jax.numpy as jnp
from jax import lax
from jax.experimental import pallas as pl
from jax.experimental.pallas import tpu as pltpu
from jax.sharding import PartitionSpec as P

LATENT_CHANNELS = 16
MIDDLE_CHANNELS = 384
OUTPUT_CHANNELS = 192
FRAMES = 4
CAPACITY = 2
EPSILON = 1e-06

ROWS = 2
WIDTH = 32
WINDOW = (ROWS + 2) * WIDTH
PATCH = 9 * LATENT_CHANNELS
SEQ = FRAMES + 2
GROUP = 2

MESH = pl.DeviceIdType.MESH
BF16 = jnp.bfloat16
F32 = jnp.float32


def pick_two(dest_ref, start, target):
    seen = jnp.int32(0)
    first = jnp.int32(0)
    second = jnp.int32(0)
    for j in range(4):
        hit = dest_ref[start + j] == target
        first = jnp.where(hit & (seen == 0), j, first)
        second = jnp.where(hit & (seen == 1), j, second)
        seen = seen + hit.astype(jnp.int32)
    return first, second, seen


def lane_join(pieces):
    return jnp.concatenate([p.astype(F32) for p in pieces], axis=-1).astype(BF16)


def exchange_kernel(
    groups,
    tiles,
    dest_ref,
    cache_slot_ref,
    latent_ref,
    latent_cache_ref,
    feature_ref,
    out_weight_ref,
    latent_out,
    cache_out,
    feature_out,
    weight_out,
    latent_send,
    cache_send,
    feature_send,
    weight_scratch,
    latent_ssem,
    latent_rsem,
    cache_ssem,
    cache_rsem,
    feature_ssem,
    feature_rsem,
    weight_sem,
):
    group = lax.axis_index("req")
    tile = lax.axis_index("tile")

    def peer(offset, turn):
        return (lax.rem(group + turn, groups), lax.rem(tile + offset + tiles, tiles))

    barrier = pltpu.get_barrier_semaphore()
    for offset in (-1, 0, 1):
        for turn in range(4):
            if offset or turn:
                pl.semaphore_signal(barrier, inc=1, device_id=peer(offset, turn), device_id_type=MESH)

    for source in range(4):
        first, second, _ = pick_two(dest_ref, 4 * source, group)
        for k, local in ((0, first), (1, second)):
            row = cache_slot_ref[4 * source + local]
            slot = 2 * source + k
            for edge in range(2):
                for f in range(2):
                    feature_send[edge, slot, f] = feature_ref[row, f, edge]
            cache_send[slot] = lane_join(
                [latent_cache_ref[row, f, y] for f in range(2) for y in range(2)]
            )
    for turn in range(4):
        first, second, _ = pick_two(dest_ref, 4 * group, lax.rem(group + turn, groups))
        for k, local in ((0, first), (1, second)):
            for pair in range(2):
                latent_send[turn, k, pair] = lane_join(
                    [latent_ref[local, 2 * pair + f, y] for f in range(2) for y in range(2)]
                )

    pl.semaphore_wait(barrier, 11)
    copies = []
    for edge, offset, place in ((1, 1, 0), (0, -1, 1)):
        copies.append(
            pltpu.make_async_remote_copy(
                src_ref=feature_send.at[edge],
                dst_ref=feature_out.at[place],
                send_sem=feature_ssem.at[place],
                recv_sem=feature_rsem.at[place],
                device_id=peer(offset, 0),
                device_id_type=MESH,
            )
        )
    for offset in (1, -1, 0):
        place = 1 - offset
        for turn in range(4):
            if offset == 0 and turn == 0:
                copies.append(
                    pltpu.make_async_copy(
                        latent_send.at[0], latent_out.at[1, 0], latent_rsem.at[1, 0]
                    )
                )
            else:
                copies.append(
                    pltpu.make_async_remote_copy(
                        src_ref=latent_send.at[turn],
                        dst_ref=latent_out.at[place, turn],
                        send_sem=latent_ssem.at[place, turn],
                        recv_sem=latent_rsem.at[place, turn],
                        device_id=peer(offset, turn),
                        device_id_type=MESH,
                    )
                )
        if offset == 0:
            copies.append(pltpu.make_async_copy(cache_send, cache_out.at[1], cache_rsem.at[1]))
        else:
            copies.append(
                pltpu.make_async_remote_copy(
                    src_ref=cache_send,
                    dst_ref=cache_out.at[place],
                    send_sem=cache_ssem.at[place],
                    recv_sem=cache_rsem.at[place],
                    device_id=peer(offset, 0),
                    device_id_type=MESH,
                )
            )
    for copy in copies:
        copy.start()

    def combine(i, carry):
        at = pl.multiple_of(i * 16, 16)
        taps = [
            [out_weight_ref[b, c, pl.ds(at, 16), :].astype(F32) for c in range(3)] for b in range(3)
        ]
        rows = (
            (taps[0], [u + v for u, v in zip(taps[1], taps[2])]),
            ([u + v for u, v in zip(taps[0], taps[1])], taps[2]),
        )
        for py in range(2):
            for ty in range(2):
                line = rows[py][ty]
                columns = ((line[0], line[1] + line[2]), (line[0] + line[1], line[2]))
                for px in range(2):
                    for tx in range(2):
                        k = (2 * ty + tx) * MIDDLE_CHANNELS
                        weight_scratch[2 * py + px, pl.ds(at, 16), k : k + MIDDLE_CHANNELS] = (
                            columns[px][tx].astype(BF16)
                        )
        return carry

    lax.fori_loop(0, OUTPUT_CHANNELS // 16, combine, 0)
    weight_copy = pltpu.make_async_copy(weight_scratch, weight_out, weight_sem)
    weight_copy.start()
    for copy in copies:
        copy.wait()
    weight_copy.wait()


def decode_kernel(
    dest_ref,
    valid_ref,
    cache_slot_ref,
    latent_ref,
    cache_ref,
    edge_ref,
    feature_ref,
    in_weight_ref,
    in_bias_ref,
    gain_ref,
    time_weight_hbm,
    time_bias_ref,
    out_weight_hbm,
    out_bias_ref,
    out_ref,
    count_ref,
    work_ref,
    patch_ref,
    seq_ref,
    shift_ref,
    low_ref,
    high_ref,
    stage_ref,
    zero_ref,
    time_weight_ref,
    out_weight_ref,
    weight_sem,
    feature_sem,
    zero_sem,
    stage_sem,
):
    group = lax.axis_index("req")
    tile = lax.axis_index("tile")
    tiles = lax.axis_size("tile")

    time_copy = pltpu.make_async_copy(time_weight_hbm, time_weight_ref, weight_sem.at[0])
    out_copy = pltpu.make_async_copy(out_weight_hbm, out_weight_ref, weight_sem.at[1])
    time_copy.start()
    out_copy.start()

    def feature_copies(slot, row):
        place = pl.ds(slot * SEQ, 2)
        return (
            pltpu.make_async_copy(
                feature_ref.at[row],
                seq_ref.at[place, WIDTH : WIDTH + ROWS * WIDTH, :],
                feature_sem.at[0, slot],
            ),
            pltpu.make_async_copy(
                edge_ref.at[0, slot], seq_ref.at[place, 0:WIDTH, :], feature_sem.at[1, slot]
            ),
            pltpu.make_async_copy(
                edge_ref.at[1, slot],
                seq_ref.at[place, WINDOW - WIDTH : WINDOW, :],
                feature_sem.at[2, slot],
            ),
        )

    total = jnp.int32(0)
    last = jnp.int32(0)
    for source in range(4):
        first, second, seen = pick_two(dest_ref, 4 * source, group)
        for k, local in ((0, first), (1, second)):
            slot = 2 * source + k
            r = 4 * source + local
            count = jnp.where(seen > k, valid_ref[r], 0)
            count_ref[slot] = count
            row = cache_slot_ref[r]
            for f in range(FRAMES):
                work_ref[total] = jnp.int32(slot * FRAMES + f)
                keep = f < count
                last = jnp.where(keep, slot * FRAMES + f, last)
                total = total + keep.astype(jnp.int32)

            @pl.when(count > 0)
            def _():
                for copy in feature_copies(slot, row):
                    copy.start()

    for extra in range(GROUP):
        work_ref[total + extra] = last

    zero_ref[...] = jnp.zeros_like(zero_ref)

    def zero_copy(i):
        return pltpu.make_async_copy(
            zero_ref, out_ref.at[i // FRAMES, pl.ds(2 * (i % FRAMES), 2)], zero_sem.at[i]
        )

    @pl.loop(0, 8 * FRAMES)
    def _(i):
        @pl.when((i % FRAMES) >= count_ref[i // FRAMES])
        def _():
            zero_copy(i).start()

    lane = lax.broadcasted_iota(jnp.int32, (LATENT_CHANNELS, 128), 1)
    column = lane % WIDTH

    @pl.loop(0, 8)
    def _(slot):
        count = count_ref[slot]

        @pl.when(count > 0)
        def _():
            turn = lax.rem(group - slot // 2 + 4, 4)
            k = slot % 2
            for pair in range(3):
                blocks = []
                for place in range(3):
                    if pair == 0:
                        block = cache_ref[place, slot].astype(F32)
                    else:
                        block = latent_ref[place, turn, k, pair - 1].astype(F32)
                        frame = 2 * (pair - 1) + lane // 64
                        block = jnp.where(frame < count, block, 0.0)
                    if place == 0:
                        block = jnp.where(tile > 0, block, 0.0)
                    if place == 2:
                        block = jnp.where(tile < tiles - 1, block, 0.0)
                    blocks.append(block)
                up, own, down = blocks

                def turned(value, by):
                    return pltpu.roll(value, by % 128, 1)

                own_half = turned(own, 64)
                windows = (
                    (
                        jnp.where(lane < 64, up, own_half),
                        jnp.where(
                            lane < 32,
                            turned(up, -32),
                            jnp.where(lane < 96, turned(own, 32), turned(down, -32)),
                        ),
                        jnp.where(lane < 64, own, turned(down, 64)),
                    ),
                    (
                        jnp.where(lane < 64, turned(up, 64), own),
                        jnp.where(
                            lane < 32,
                            turned(up, 32),
                            jnp.where(lane < 96, turned(own, -32), turned(down, 32)),
                        ),
                        jnp.where(lane < 64, own_half, down),
                    ),
                )
                for half in range(2):
                    base = (slot * SEQ + 2 * pair + half) * PATCH
                    for b in range(3):
                        window = windows[half][b]
                        shifted = (
                            jnp.where(column == 0, 0.0, turned(window, 1)),
                            window,
                            jnp.where(column == WIDTH - 1, 0.0, turned(window, -1)),
                        )
                        for c in range(3):
                            at = pl.multiple_of(base + (3 * b + c) * 16, 16)
                            patch_ref[pl.ds(at, 16), :] = shifted[c].astype(BF16)

    steps = (total + GROUP - 1) // GROUP

    @pl.loop(0, steps)
    def _(step):
        places = []
        pieces = []
        for u in range(GROUP):
            item = work_ref[step * GROUP + u]
            place = (item // FRAMES) * SEQ + item % FRAMES
            places.append(place)
            at = pl.multiple_of(place * PATCH, 16)
            pieces.append(patch_ref[pl.ds(at, 3 * PATCH), :])
        stacked = jnp.concatenate(pieces, axis=1)
        inner = (
            lax.dot_general(
                stacked,
                in_weight_ref[...],
                (((0,), (0,)), ((), ())),
                preferred_element_type=F32,
            )
            + in_bias_ref[...]
        )
        scale = lax.rsqrt(jnp.mean(inner * inner, axis=-1, keepdims=True) + EPSILON)
        active = jax.nn.silu(inner * scale * gain_ref[...]).astype(BF16)
        for u in range(GROUP):
            seq_ref[places[u] + 2] = active[u * WINDOW : (u + 1) * WINDOW]

    for slot in range(8):

        @pl.when(count_ref[slot] > 0)
        def _():
            for copy in feature_copies(slot, 0):
                copy.wait()

    time_copy.wait()
    out_copy.wait()

    pixel = lax.broadcasted_iota(jnp.int32, (WINDOW, 2 * MIDDLE_CHANNELS), 0)
    inside = ((pixel >= WIDTH) | (tile > 0)) & ((pixel < WINDOW - WIDTH) | (tile < tiles - 1))
    pixel_column = pixel % WIDTH

    def stage_copy(buffer, u, item):
        return pltpu.make_async_copy(
            stage_ref.at[buffer, u],
            out_ref.at[item // FRAMES, pl.ds(2 * (item % FRAMES), 2)],
            stage_sem.at[buffer, u],
        )

    @pl.loop(0, steps)
    def _(step):
        buffer = step % 2
        items = [work_ref[step * GROUP + u] for u in range(GROUP)]
        rows = []
        for u in range(GROUP):
            place = (items[u] // FRAMES) * SEQ + items[u] % FRAMES
            rows.append(jnp.concatenate([seq_ref[place + a] for a in range(3)], axis=1))
        doubled = (
            jnp.dot(
                jnp.concatenate(rows, axis=0), time_weight_ref[...], preferred_element_type=F32
            )
            + time_bias_ref[...]
        )
        for u in range(GROUP):
            own = doubled[u * WINDOW : (u + 1) * WINDOW].astype(BF16).astype(F32)
            own = jnp.where(inside, own, 0.0)
            before = jnp.where(pixel_column == 0, 0.0, pltpu.roll(own, 1, 0))
            after = jnp.where(pixel_column == WIDTH - 1, 0.0, pltpu.roll(own, WINDOW - 1, 0))
            for c, value in enumerate((before, own, after)):
                value = value.astype(BF16)
                for h in range(2):
                    shift_ref[c, 2 * u + h] = value[:, h * MIDDLE_CHANNELS : (h + 1) * MIDDLE_CHANNELS]

        for py in range(2):
            for px in range(2):
                taps = []
                for ty in range(2):
                    for tx in range(2):
                        a = (py + ty) * WIDTH
                        taps.append(
                            shift_ref[px + tx, :, a : a + ROWS * WIDTH, :].reshape(
                                2 * GROUP * ROWS * WIDTH, MIDDLE_CHANNELS
                            )
                        )
                result = (
                    lax.dot_general(
                        jnp.concatenate(taps, axis=1),
                        out_weight_ref[2 * py + px],
                        (((1,), (1,)), ((), ())),
                        preferred_element_type=F32,
                    )
                    + out_bias_ref[...]
                )
                for q in range(2 * GROUP):
                    for y in range(ROWS):
                        at = (q * ROWS + y) * WIDTH
                        spread = pl.ds(px, WIDTH, stride=2)
                        part = result[at : at + WIDTH]
                        low_ref[q, 2 * y + py, spread, :] = part[:, :128]
                        high_ref[q, 2 * y + py, spread, 0 : OUTPUT_CHANNELS - 128] = part[:, 128:]

        @pl.when(step >= 2)
        def _():
            for u in range(GROUP):
                stage_copy(buffer, u, 0).wait()

        for u in range(GROUP):
            stage_ref[buffer, u, :, :, :, 0:128] = low_ref[2 * u : 2 * u + 2].astype(BF16)
            stage_ref[buffer, u, :, :, :, 128:OUTPUT_CHANNELS] = high_ref[
                2 * u : 2 * u + 2, :, :, 0 : OUTPUT_CHANNELS - 128
            ].astype(BF16)
            if u == 0:
                stage_copy(buffer, u, items[u]).start()
            else:

                @pl.when(step * GROUP + u < total)
                def _():
                    stage_copy(buffer, u, items[u]).start()

    for back in range(2, 0, -1):

        @pl.when(steps >= back)
        def _():
            step = steps - back
            for u in range(GROUP):

                @pl.when(step * GROUP + u < total)
                def _():
                    stage_copy(step % 2, u, 0).wait()

    @pl.loop(0, 8 * FRAMES)
    def _(i):
        @pl.when((i % FRAMES) >= count_ref[i // FRAMES])
        def _():
            zero_copy(i).wait()


def per_device(
    latent,
    destination,
    valid_frames,
    cache_slot,
    latent_cache,
    feature_cache,
    in_weight,
    in_bias,
    norm_gain,
    time_weight,
    time_bias,
    out_weight,
    out_bias,
):
    groups = lax.axis_size("req")
    tiles = lax.axis_size("tile")
    target = destination[:, 0]
    smem = pl.BlockSpec(memory_space=pltpu.SMEM)
    vmem = pl.BlockSpec(memory_space=pltpu.VMEM)
    hbm = pl.BlockSpec(memory_space=pl.ANY)
    shape = jax.ShapeDtypeStruct
    dma = pltpu.SemaphoreType.DMA
    slots = 8

    latents, cached, edges, phase_weight = pl.pallas_call(
        functools.partial(exchange_kernel, groups, tiles),
        out_shape=(
            shape((3, 4, CAPACITY, 2, LATENT_CHANNELS, 128), BF16),
            shape((3, slots, LATENT_CHANNELS, 128), BF16),
            shape((2, slots, 2, WIDTH, MIDDLE_CHANNELS), BF16),
            shape((4, OUTPUT_CHANNELS, 4 * MIDDLE_CHANNELS), BF16),
        ),
        in_specs=[smem, smem, vmem, vmem, vmem, vmem],
        out_specs=(hbm, hbm, hbm, hbm),
        scratch_shapes=[
            pltpu.VMEM((4, CAPACITY, 2, LATENT_CHANNELS, 128), BF16),
            pltpu.VMEM((slots, LATENT_CHANNELS, 128), BF16),
            pltpu.VMEM((2, slots, 2, WIDTH, MIDDLE_CHANNELS), BF16),
            pltpu.VMEM((4, OUTPUT_CHANNELS, 4 * MIDDLE_CHANNELS), BF16),
            dma((3, 4)),
            dma((3, 4)),
            dma((3,)),
            dma((3,)),
            dma((2,)),
            dma((2,)),
            dma(()),
        ],
        compiler_params=pltpu.CompilerParams(
            collective_id=0, has_side_effects=True, vmem_limit_bytes=40 * 2**20
        ),
        name="exchange",
    )(
        target,
        cache_slot,
        jnp.transpose(latent, (0, 1, 2, 4, 3)),
        jnp.transpose(latent_cache, (0, 1, 2, 4, 3)),
        feature_cache,
        jnp.transpose(out_weight, (0, 1, 3, 2)),
    )

    return pl.pallas_call(
        decode_kernel,
        out_shape=shape((slots, 2 * FRAMES, 2 * ROWS, 2 * WIDTH, OUTPUT_CHANNELS), BF16),
        in_specs=[smem, smem, smem, vmem, vmem, hbm, hbm, vmem, vmem, vmem, hbm, vmem, hbm, vmem],
        out_specs=hbm,
        scratch_shapes=[
            pltpu.SMEM((slots,), jnp.int32),
            pltpu.SMEM((slots * FRAMES + GROUP,), jnp.int32),
            pltpu.VMEM((slots * SEQ * PATCH, WINDOW), BF16),
            pltpu.VMEM((slots * SEQ, WINDOW, MIDDLE_CHANNELS), BF16),
            pltpu.VMEM((3, 2 * GROUP, WINDOW, MIDDLE_CHANNELS), BF16),
            pltpu.VMEM((2 * GROUP, 2 * ROWS, 2 * WIDTH, 128), F32),
            pltpu.VMEM((2 * GROUP, 2 * ROWS, 2 * WIDTH, 128), F32),
            pltpu.VMEM((2, GROUP, 2, 2 * ROWS, 2 * WIDTH, OUTPUT_CHANNELS), BF16),
            pltpu.VMEM((2, 2 * ROWS, 2 * WIDTH, OUTPUT_CHANNELS), BF16),
            pltpu.VMEM((3 * MIDDLE_CHANNELS, 2 * MIDDLE_CHANNELS), BF16),
            pltpu.VMEM((4, OUTPUT_CHANNELS, 4 * MIDDLE_CHANNELS), BF16),
            dma((2,)),
            dma((3, slots)),
            dma((slots * FRAMES,)),
            dma((2, GROUP)),
        ],
        compiler_params=pltpu.CompilerParams(vmem_limit_bytes=56 * 2**20),
        name="decode",
    )(
        target,
        valid_frames,
        cache_slot,
        latents,
        cached,
        edges,
        feature_cache.reshape(16, 2, ROWS * WIDTH, MIDDLE_CHANNELS),
        in_weight.reshape(27 * LATENT_CHANNELS, MIDDLE_CHANNELS),
        in_bias.reshape(1, -1),
        norm_gain.reshape(1, -1),
        time_weight.reshape(3 * MIDDLE_CHANNELS, 2 * MIDDLE_CHANNELS),
        time_bias.reshape(1, -1),
        phase_weight,
        out_bias.reshape(1, -1),
    )


def solution(mesh):
    placed = (
        P("req", None, "tile", None, None),
        P(),
        P(),
        P(),
        P("req", None, "tile", None, None),
        P("req", None, "tile", None, None),
        P(),
        P(),
        P(),
        P(),
        P(),
        P(),
        P(),
    )
    return jax.shard_map(
        per_device,
        mesh=mesh,
        in_specs=placed,
        out_specs=P("req", None, "tile", None, None),
        check_vma=False,
    )
```

```python
import functools

import jax
import jax.numpy as jnp
from jax import lax
from jax.experimental import pallas as pl
from jax.experimental.pallas import tpu as pltpu
from jax.sharding import PartitionSpec as P

LATENT_CHANNELS = 16
MIDDLE_CHANNELS = 384
OUTPUT_CHANNELS = 192
FRAMES = 4
CAPACITY = 2
EPSILON = 1e-06

ROWS = 2
WIDTH = 32
WINDOW = (ROWS + 2) * WIDTH
PATCH = 9 * LATENT_CHANNELS
SEQ = FRAMES + 2
GROUP = 2
VMEM_LIMIT = 63 * 2**20

MESH = pl.DeviceIdType.MESH
BF16 = jnp.bfloat16
F32 = jnp.float32


def pick_two(dest_ref, start, target):
    seen = jnp.int32(0)
    first = jnp.int32(0)
    second = jnp.int32(0)
    for j in range(4):
        hit = dest_ref[start + j] == target
        first = jnp.where(hit & (seen == 0), j, first)
        second = jnp.where(hit & (seen == 1), j, second)
        seen = seen + hit.astype(jnp.int32)
    return first, second, seen


def lane_join(pieces):
    return jnp.concatenate([p.astype(F32) for p in pieces], axis=-1).astype(BF16)


def exchange_kernel(
    groups,
    tiles,
    dest_ref,
    cache_slot_ref,
    latent_hbm,
    latent_cache_hbm,
    feature_hbm,
    out_weight_hbm,
    latent_out,
    cache_out,
    feature_out,
    weight_out,
    latent_ref,
    latent_cache_ref,
    feature_ref,
    out_weight_ref,
    latent_send,
    cache_send,
    feature_send,
    weight_scratch,
    latent_ssem,
    latent_rsem,
    cache_ssem,
    cache_rsem,
    feature_ssem,
    feature_rsem,
    weight_sem,
    load_sem,
):
    group = lax.axis_index("req")
    tile = lax.axis_index("tile")
    loads = [
        pltpu.make_async_copy(source, target, load_sem.at[i])
        for i, (source, target) in enumerate(
            (
                (feature_hbm, feature_ref),
                (latent_cache_hbm, latent_cache_ref),
                (latent_hbm, latent_ref),
                (out_weight_hbm, out_weight_ref),
            )
        )
    ]
    for load in loads:
        load.start()

    def peer(offset, turn):
        return (lax.rem(group + turn, groups), lax.rem(tile + offset + tiles, tiles))

    barrier = pltpu.get_barrier_semaphore()
    for offset in (-1, 0, 1):
        for turn in range(4):
            if offset or turn:
                pl.semaphore_signal(barrier, inc=1, device_id=peer(offset, turn), device_id_type=MESH)

    for load in loads[:3]:
        load.wait()
    for source in range(4):
        first, second, _ = pick_two(dest_ref, 4 * source, group)
        for k, local in ((0, first), (1, second)):
            row = cache_slot_ref[4 * source + local]
            slot = 2 * source + k
            for edge in range(2):
                for f in range(2):
                    feature_send[edge, slot, f] = feature_ref[row, f, edge]
            cache_send[slot] = lane_join(
                [latent_cache_ref[row, f, y] for f in range(2) for y in range(2)]
            )
    for turn in range(4):
        first, second, _ = pick_two(dest_ref, 4 * group, lax.rem(group + turn, groups))
        for k, local in ((0, first), (1, second)):
            for pair in range(2):
                latent_send[turn, k, pair] = lane_join(
                    [latent_ref[local, 2 * pair + f, y] for f in range(2) for y in range(2)]
                )

    pl.semaphore_wait(barrier, 11)
    copies = []
    for edge, offset, place in ((1, 1, 0), (0, -1, 1)):
        copies.append(
            pltpu.make_async_remote_copy(
                src_ref=feature_send.at[edge],
                dst_ref=feature_out.at[place],
                send_sem=feature_ssem.at[place],
                recv_sem=feature_rsem.at[place],
                device_id=peer(offset, 0),
                device_id_type=MESH,
            )
        )
    for offset in (1, -1, 0):
        place = 1 - offset
        for turn in range(4):
            if offset == 0 and turn == 0:
                copies.append(
                    pltpu.make_async_copy(
                        latent_send.at[0], latent_out.at[1, 0], latent_rsem.at[1, 0]
                    )
                )
            else:
                copies.append(
                    pltpu.make_async_remote_copy(
                        src_ref=latent_send.at[turn],
                        dst_ref=latent_out.at[place, turn],
                        send_sem=latent_ssem.at[place, turn],
                        recv_sem=latent_rsem.at[place, turn],
                        device_id=peer(offset, turn),
                        device_id_type=MESH,
                    )
                )
        if offset == 0:
            copies.append(pltpu.make_async_copy(cache_send, cache_out.at[1], cache_rsem.at[1]))
        else:
            copies.append(
                pltpu.make_async_remote_copy(
                    src_ref=cache_send,
                    dst_ref=cache_out.at[place],
                    send_sem=cache_ssem.at[place],
                    recv_sem=cache_rsem.at[place],
                    device_id=peer(offset, 0),
                    device_id_type=MESH,
                )
            )
    for copy in copies:
        copy.start()
    loads[3].wait()

    def combine(i, carry):
        at = pl.multiple_of(i * 16, 16)
        taps = [
            [out_weight_ref[b, c, pl.ds(at, 16), :].astype(F32) for c in range(3)] for b in range(3)
        ]
        rows = (
            (taps[0], [u + v for u, v in zip(taps[1], taps[2])]),
            ([u + v for u, v in zip(taps[0], taps[1])], taps[2]),
        )
        for py in range(2):
            for ty in range(2):
                line = rows[py][ty]
                columns = ((line[0], line[1] + line[2]), (line[0] + line[1], line[2]))
                for px in range(2):
                    for tx in range(2):
                        k = (2 * ty + tx) * MIDDLE_CHANNELS
                        weight_scratch[2 * py + px, pl.ds(at, 16), k : k + MIDDLE_CHANNELS] = (
                            columns[px][tx].astype(BF16)
                        )
        return carry

    lax.fori_loop(0, OUTPUT_CHANNELS // 16, combine, 0)
    weight_copy = pltpu.make_async_copy(weight_scratch, weight_out, weight_sem)
    weight_copy.start()
    for copy in copies:
        copy.wait()
    weight_copy.wait()


def decode_kernel(
    dest_ref,
    valid_ref,
    cache_slot_ref,
    latent_ref,
    cache_ref,
    edge_ref,
    feature_ref,
    in_weight_ref,
    in_bias_ref,
    gain_ref,
    time_weight_hbm,
    time_bias_ref,
    out_weight_hbm,
    out_bias_ref,
    out_ref,
    count_ref,
    work_ref,
    patch_ref,
    seq_ref,
    shift_ref,
    low_ref,
    high_ref,
    stage_ref,
    zero_ref,
    time_weight_ref,
    out_weight_ref,
    weight_sem,
    feature_sem,
    zero_sem,
    stage_sem,
):
    group = lax.axis_index("req")
    tile = lax.axis_index("tile")
    tiles = lax.axis_size("tile")

    time_copy = pltpu.make_async_copy(time_weight_hbm, time_weight_ref, weight_sem.at[0])
    out_copy = pltpu.make_async_copy(out_weight_hbm, out_weight_ref, weight_sem.at[1])
    time_copy.start()
    out_copy.start()

    def feature_copies(slot, row):
        place = pl.ds(slot * SEQ, 2)
        return (
            pltpu.make_async_copy(
                feature_ref.at[row],
                seq_ref.at[place, WIDTH : WIDTH + ROWS * WIDTH, :],
                feature_sem.at[0, slot],
            ),
            pltpu.make_async_copy(
                edge_ref.at[0, slot], seq_ref.at[place, 0:WIDTH, :], feature_sem.at[1, slot]
            ),
            pltpu.make_async_copy(
                edge_ref.at[1, slot],
                seq_ref.at[place, WINDOW - WIDTH : WINDOW, :],
                feature_sem.at[2, slot],
            ),
        )

    total = jnp.int32(0)
    last = jnp.int32(0)
    for source in range(4):
        first, second, seen = pick_two(dest_ref, 4 * source, group)
        for k, local in ((0, first), (1, second)):
            slot = 2 * source + k
            r = 4 * source + local
            count = jnp.where(seen > k, valid_ref[r], 0)
            count_ref[slot] = count
            row = cache_slot_ref[r]
            for f in range(FRAMES):
                work_ref[total] = jnp.int32(slot * FRAMES + f)
                keep = f < count
                last = jnp.where(keep, slot * FRAMES + f, last)
                total = total + keep.astype(jnp.int32)

            @pl.when(count > 0)
            def _():
                for copy in feature_copies(slot, row):
                    copy.start()

    for extra in range(GROUP):
        work_ref[total + extra] = last

    zero_ref[...] = jnp.zeros_like(zero_ref)

    def zero_copy(i):
        return pltpu.make_async_copy(
            zero_ref, out_ref.at[i // FRAMES, pl.ds(2 * (i % FRAMES), 2)], zero_sem.at[i]
        )

    @pl.loop(0, 8 * FRAMES)
    def _(i):
        @pl.when((i % FRAMES) >= count_ref[i // FRAMES])
        def _():
            zero_copy(i).start()

    lane = lax.broadcasted_iota(jnp.int32, (LATENT_CHANNELS, 128), 1)
    column = lane % WIDTH

    @pl.loop(0, 8)
    def _(slot):
        count = count_ref[slot]

        @pl.when(count > 0)
        def _():
            turn = lax.rem(group - slot // 2 + 4, 4)
            k = slot % 2
            for pair in range(3):
                blocks = []
                for place in range(3):
                    if pair == 0:
                        block = cache_ref[place, slot].astype(F32)
                    else:
                        block = latent_ref[place, turn, k, pair - 1].astype(F32)
                        frame = 2 * (pair - 1) + lane // 64
                        block = jnp.where(frame < count, block, 0.0)
                    if place == 0:
                        block = jnp.where(tile > 0, block, 0.0)
                    if place == 2:
                        block = jnp.where(tile < tiles - 1, block, 0.0)
                    blocks.append(block)
                up, own, down = blocks

                def turned(value, by):
                    return pltpu.roll(value, by % 128, 1)

                own_half = turned(own, 64)
                windows = (
                    (
                        jnp.where(lane < 64, up, own_half),
                        jnp.where(
                            lane < 32,
                            turned(up, -32),
                            jnp.where(lane < 96, turned(own, 32), turned(down, -32)),
                        ),
                        jnp.where(lane < 64, own, turned(down, 64)),
                    ),
                    (
                        jnp.where(lane < 64, turned(up, 64), own),
                        jnp.where(
                            lane < 32,
                            turned(up, 32),
                            jnp.where(lane < 96, turned(own, -32), turned(down, 32)),
                        ),
                        jnp.where(lane < 64, own_half, down),
                    ),
                )
                for half in range(2):
                    base = (slot * SEQ + 2 * pair + half) * PATCH
                    for b in range(3):
                        window = windows[half][b]
                        shifted = (
                            jnp.where(column == 0, 0.0, turned(window, 1)),
                            window,
                            jnp.where(column == WIDTH - 1, 0.0, turned(window, -1)),
                        )
                        for c in range(3):
                            at = pl.multiple_of(base + (3 * b + c) * 16, 16)
                            patch_ref[pl.ds(at, 16), :] = shifted[c].astype(BF16)

    steps = (total + GROUP - 1) // GROUP

    @pl.loop(0, steps)
    def _(step):
        places = []
        pieces = []
        for u in range(GROUP):
            item = work_ref[step * GROUP + u]
            place = (item // FRAMES) * SEQ + item % FRAMES
            places.append(place)
            at = pl.multiple_of(place * PATCH, 16)
            pieces.append(patch_ref[pl.ds(at, 3 * PATCH), :])
        stacked = jnp.concatenate(pieces, axis=1)
        inner = (
            lax.dot_general(
                stacked,
                in_weight_ref[...],
                (((0,), (0,)), ((), ())),
                preferred_element_type=F32,
            )
            + in_bias_ref[...][None, :]
        )
        scale = lax.rsqrt(jnp.mean(inner * inner, axis=-1, keepdims=True) + EPSILON)
        active = jax.nn.silu(inner * scale * gain_ref[...][None, :]).astype(BF16)
        for u in range(GROUP):
            seq_ref[places[u] + 2] = active[u * WINDOW : (u + 1) * WINDOW]

    for slot in range(8):

        @pl.when(count_ref[slot] > 0)
        def _():
            for copy in feature_copies(slot, 0):
                copy.wait()

    time_copy.wait()
    out_copy.wait()

    pixel = lax.broadcasted_iota(jnp.int32, (WINDOW, 2 * MIDDLE_CHANNELS), 0)
    inside = ((pixel >= WIDTH) | (tile > 0)) & ((pixel < WINDOW - WIDTH) | (tile < tiles - 1))
    pixel_column = pixel % WIDTH

    def stage_copy(buffer, u, item):
        return pltpu.make_async_copy(
            stage_ref.at[buffer, u],
            out_ref.at[item // FRAMES, pl.ds(2 * (item % FRAMES), 2)],
            stage_sem.at[buffer, u],
        )

    @pl.loop(0, steps)
    def _(step):
        buffer = step % 2
        items = [work_ref[step * GROUP + u] for u in range(GROUP)]
        rows = []
        for u in range(GROUP):
            place = (items[u] // FRAMES) * SEQ + items[u] % FRAMES
            rows.append(jnp.concatenate([seq_ref[place + a] for a in range(3)], axis=1))
        doubled = (
            jnp.dot(
                jnp.concatenate(rows, axis=0), time_weight_ref[...], preferred_element_type=F32
            )
            + time_bias_ref[...][None, :]
        )
        for u in range(GROUP):
            own = doubled[u * WINDOW : (u + 1) * WINDOW].astype(BF16).astype(F32)
            own = jnp.where(inside, own, 0.0)
            before = jnp.where(pixel_column == 0, 0.0, pltpu.roll(own, 1, 0))
            after = jnp.where(pixel_column == WIDTH - 1, 0.0, pltpu.roll(own, WINDOW - 1, 0))
            for c, value in enumerate((before, own, after)):
                value = value.astype(BF16)
                for h in range(2):
                    shift_ref[c, 2 * u + h] = value[:, h * MIDDLE_CHANNELS : (h + 1) * MIDDLE_CHANNELS]

        for py in range(2):
            for px in range(2):
                taps = []
                for ty in range(2):
                    for tx in range(2):
                        a = (py + ty) * WIDTH
                        taps.append(
                            shift_ref[px + tx, :, a : a + ROWS * WIDTH, :].reshape(
                                2 * GROUP * ROWS * WIDTH, MIDDLE_CHANNELS
                            )
                        )
                result = (
                    lax.dot_general(
                        jnp.concatenate(taps, axis=1),
                        out_weight_ref[2 * py + px],
                        (((1,), (1,)), ((), ())),
                        preferred_element_type=F32,
                    )
                    + out_bias_ref[...][None, :]
                )
                for q in range(2 * GROUP):
                    for y in range(ROWS):
                        at = (q * ROWS + y) * WIDTH
                        spread = pl.ds(px, WIDTH, stride=2)
                        part = result[at : at + WIDTH]
                        low_ref[q, 2 * y + py, spread, :] = part[:, :128]
                        high_ref[q, 2 * y + py, spread, 0 : OUTPUT_CHANNELS - 128] = part[:, 128:]

        @pl.when(step >= 2)
        def _():
            for u in range(GROUP):
                stage_copy(buffer, u, 0).wait()

        for u in range(GROUP):
            stage_ref[buffer, u, :, :, :, 0:128] = low_ref[2 * u : 2 * u + 2].astype(BF16)
            stage_ref[buffer, u, :, :, :, 128:OUTPUT_CHANNELS] = high_ref[
                2 * u : 2 * u + 2, :, :, 0 : OUTPUT_CHANNELS - 128
            ].astype(BF16)
            if u == 0:
                stage_copy(buffer, u, items[u]).start()
            else:

                @pl.when(step * GROUP + u < total)
                def _():
                    stage_copy(buffer, u, items[u]).start()

    for back in range(2, 0, -1):

        @pl.when(steps >= back)
        def _():
            step = steps - back
            for u in range(GROUP):

                @pl.when(step * GROUP + u < total)
                def _():
                    stage_copy(step % 2, u, 0).wait()

    @pl.loop(0, 8 * FRAMES)
    def _(i):
        @pl.when((i % FRAMES) >= count_ref[i // FRAMES])
        def _():
            zero_copy(i).wait()


def per_device(
    latent,
    destination,
    valid_frames,
    cache_slot,
    latent_cache,
    feature_cache,
    in_weight,
    in_bias,
    norm_gain,
    time_weight,
    time_bias,
    out_weight,
    out_bias,
):
    groups = lax.axis_size("req")
    tiles = lax.axis_size("tile")
    target = destination[:, 0]
    smem = pl.BlockSpec(memory_space=pltpu.SMEM)
    vmem = pl.BlockSpec(memory_space=pltpu.VMEM)
    hbm = pl.BlockSpec(memory_space=pl.ANY)
    shape = jax.ShapeDtypeStruct
    dma = pltpu.SemaphoreType.DMA
    slots = 8

    latents, cached, edges, phase_weight = pl.pallas_call(
        functools.partial(exchange_kernel, groups, tiles),
        out_shape=(
            shape((3, 4, CAPACITY, 2, LATENT_CHANNELS, 128), BF16),
            shape((3, slots, LATENT_CHANNELS, 128), BF16),
            shape((2, slots, 2, WIDTH, MIDDLE_CHANNELS), BF16),
            shape((4, OUTPUT_CHANNELS, 4 * MIDDLE_CHANNELS), BF16),
        ),
        in_specs=[smem, smem, hbm, hbm, hbm, hbm],
        out_specs=(hbm, hbm, hbm, hbm),
        scratch_shapes=[
            pltpu.VMEM((4, FRAMES, ROWS, LATENT_CHANNELS, WIDTH), BF16),
            pltpu.VMEM((16, 2, ROWS, LATENT_CHANNELS, WIDTH), BF16),
            pltpu.VMEM((16, 2, ROWS, WIDTH, MIDDLE_CHANNELS), BF16),
            pltpu.VMEM((3, 3, OUTPUT_CHANNELS, MIDDLE_CHANNELS), BF16),
            pltpu.VMEM((4, CAPACITY, 2, LATENT_CHANNELS, 128), BF16),
            pltpu.VMEM((slots, LATENT_CHANNELS, 128), BF16),
            pltpu.VMEM((2, slots, 2, WIDTH, MIDDLE_CHANNELS), BF16),
            pltpu.VMEM((4, OUTPUT_CHANNELS, 4 * MIDDLE_CHANNELS), BF16),
            dma((3, 4)),
            dma((3, 4)),
            dma((3,)),
            dma((3,)),
            dma((2,)),
            dma((2,)),
            dma(()),
            dma((4,)),
        ],
        compiler_params=pltpu.CompilerParams(
            collective_id=0, has_side_effects=True, vmem_limit_bytes=VMEM_LIMIT
        ),
        name="exchange",
    )(
        target,
        cache_slot,
        jnp.transpose(latent, (0, 1, 2, 4, 3)),
        jnp.transpose(latent_cache, (0, 1, 2, 4, 3)),
        feature_cache,
        jnp.transpose(out_weight, (0, 1, 3, 2)),
    )

    return pl.pallas_call(
        decode_kernel,
        out_shape=shape((slots, 2 * FRAMES, 2 * ROWS, 2 * WIDTH, OUTPUT_CHANNELS), BF16),
        in_specs=[smem, smem, smem, vmem, vmem, hbm, hbm, vmem, vmem, vmem, hbm, vmem, hbm, vmem],
        out_specs=hbm,
        scratch_shapes=[
            pltpu.SMEM((slots,), jnp.int32),
            pltpu.SMEM((slots * FRAMES + GROUP,), jnp.int32),
            pltpu.VMEM((slots * SEQ * PATCH, WINDOW), BF16),
            pltpu.VMEM((slots * SEQ, WINDOW, MIDDLE_CHANNELS), BF16),
            pltpu.VMEM((3, 2 * GROUP, WINDOW, MIDDLE_CHANNELS), BF16),
            pltpu.VMEM((2 * GROUP, 2 * ROWS, 2 * WIDTH, 128), F32),
            pltpu.VMEM((2 * GROUP, 2 * ROWS, 2 * WIDTH, 128), F32),
            pltpu.VMEM((2, GROUP, 2, 2 * ROWS, 2 * WIDTH, OUTPUT_CHANNELS), BF16),
            pltpu.VMEM((2, 2 * ROWS, 2 * WIDTH, OUTPUT_CHANNELS), BF16),
            pltpu.VMEM((3 * MIDDLE_CHANNELS, 2 * MIDDLE_CHANNELS), BF16),
            pltpu.VMEM((4, OUTPUT_CHANNELS, 4 * MIDDLE_CHANNELS), BF16),
            dma((2,)),
            dma((3, slots)),
            dma((slots * FRAMES,)),
            dma((2, GROUP)),
        ],
        compiler_params=pltpu.CompilerParams(vmem_limit_bytes=VMEM_LIMIT),
        name="decode",
    )(
        target,
        valid_frames,
        cache_slot,
        latents,
        cached,
        edges,
        feature_cache.reshape(16, 2, ROWS * WIDTH, MIDDLE_CHANNELS),
        in_weight.reshape(27 * LATENT_CHANNELS, MIDDLE_CHANNELS),
        in_bias,
        norm_gain,
        time_weight.reshape(3 * MIDDLE_CHANNELS, 2 * MIDDLE_CHANNELS),
        time_bias,
        phase_weight,
        out_bias,
    )


def solution(mesh):
    placed = (
        P("req", None, "tile", None, None),
        P(),
        P(),
        P(),
        P("req", None, "tile", None, None),
        P("req", None, "tile", None, None),
        P(),
        P(),
        P(),
        P(),
        P(),
        P(),
        P(),
    )
    return jax.shard_map(
        per_device,
        mesh=mesh,
        in_specs=placed,
        out_specs=P("req", None, "tile", None, None),
        check_vma=False,
    )
```

```python
import functools

import jax
import jax.numpy as jnp
from jax import lax
from jax.experimental import pallas as pl
from jax.experimental.pallas import tpu as pltpu
from jax.sharding import PartitionSpec as P

LATENT_CHANNELS = 16
MIDDLE_CHANNELS = 384
OUTPUT_CHANNELS = 192
FRAMES = 4
CAPACITY = 2
EPSILON = 1e-06

ROWS = 2
WIDTH = 32
WINDOW = (ROWS + 2) * WIDTH
PATCH = 9 * LATENT_CHANNELS
SEQ = FRAMES + 2
GROUP = 4
VMEM_LIMIT = 28 * 2**20

MESH = pl.DeviceIdType.MESH
BF16 = jnp.bfloat16
F32 = jnp.float32


def pick_two(dest_ref, start, target):
    seen = jnp.int32(0)
    first = jnp.int32(0)
    second = jnp.int32(0)
    for j in range(4):
        hit = dest_ref[start + j] == target
        first = jnp.where(hit & (seen == 0), j, first)
        second = jnp.where(hit & (seen == 1), j, second)
        seen = seen + hit.astype(jnp.int32)
    return first, second, seen


def lane_join(pieces):
    return jnp.concatenate([p.astype(F32) for p in pieces], axis=-1).astype(BF16)


def exchange_kernel(
    groups,
    tiles,
    dest_hbm,
    valid_hbm,
    cache_slot_hbm,
    latent_hbm,
    latent_cache_hbm,
    feature_hbm,
    out_weight_hbm,
    cached_ref,
    patch_ref,
    phase_ref,
    dest_ref,
    valid_ref,
    cache_slot_ref,
    latent_ref,
    latent_cache_ref,
    feature_ref,
    out_weight_ref,
    latent_send,
    cache_send,
    feature_send,
    latent_recv,
    cache_recv,
    count_ref,
    latent_ssem,
    latent_rsem,
    cache_ssem,
    cache_rsem,
    feature_ssem,
    feature_rsem,
    load_sem,
):
    group = lax.axis_index("req")
    tile = lax.axis_index("tile")
    loads = [
        pltpu.make_async_copy(source, target, load_sem.at[i])
        for i, (source, target) in enumerate(
            (
                (dest_hbm, dest_ref),
                (cache_slot_hbm, cache_slot_ref),
                (valid_hbm, valid_ref),
                (latent_hbm, latent_ref),
                (latent_cache_hbm, latent_cache_ref),
                (feature_hbm, feature_ref),
                (out_weight_hbm, out_weight_ref),
            )
        )
    ]
    for load in loads:
        load.start()

    def peer(offset, turn):
        return (lax.rem(group + turn, groups), lax.rem(tile + offset + tiles, tiles))

    present = {-1: tile > 0, 0: None, 1: tile < tiles - 1}

    def where_present(offset, act):
        def run():
            act()

        if offset == 0:
            run()
        else:
            pl.when(present[offset])(run)

    barrier = pltpu.get_barrier_semaphore()
    for offset in (-1, 0, 1):

        def greet():
            for turn in range(4):
                if offset or turn:
                    pl.semaphore_signal(
                        barrier, inc=1, device_id=peer(offset, turn), device_id_type=MESH
                    )

        where_present(offset, greet)

    for load in loads[:3]:
        load.wait()

    cache_rows = []
    for source in range(4):
        first, second, seen = pick_two(dest_ref, 4 * source, group)
        for k, local in ((0, first), (1, second)):
            r = 4 * source + local
            cache_rows.append(cache_slot_ref[r])
            count_ref[2 * source + k] = jnp.where(seen > k, valid_ref[r], 0)
    picks = [
        pick_two(dest_ref, 4 * group, lax.rem(group + turn, groups))[:2] for turn in range(4)
    ]

    loads[3].wait()
    for turn in range(4):
        for k in range(CAPACITY):
            for pair in range(2):
                block = lane_join(
                    [latent_ref[picks[turn][k], 2 * pair + f, y] for f in range(2) for y in range(2)]
                )
                latent_send[turn, k, pair] = block
                if turn == 0:
                    latent_recv[1, 0, k, pair] = block
    loads[4].wait()
    for slot in range(8):
        block = lane_join(
            [latent_cache_ref[cache_rows[slot], f, y] for f in range(2) for y in range(2)]
        )
        cache_send[slot] = block
        cache_recv[1, slot] = block

    sides = (tile > 0).astype(jnp.int32) + (tile < tiles - 1).astype(jnp.int32)
    pl.semaphore_wait(barrier, 3 + 4 * sides)
    sends = {}
    arrivals = {}
    for offset in (1, -1, 0):
        place = 1 - offset
        sends[offset] = []
        if offset:
            sends[offset].append(
                pltpu.make_async_remote_copy(
                    src_ref=cache_send,
                    dst_ref=cache_recv.at[place],
                    send_sem=cache_ssem.at[place],
                    recv_sem=cache_rsem.at[place],
                    device_id=peer(offset, 0),
                    device_id_type=MESH,
                )
            )
        for turn in range(4):
            if offset or turn:
                sends[offset].append(
                    pltpu.make_async_remote_copy(
                        src_ref=latent_send.at[turn],
                        dst_ref=latent_recv.at[place, turn],
                        send_sem=latent_ssem.at[place, turn],
                        recv_sem=latent_rsem.at[place, turn],
                        device_id=peer(offset, turn),
                        device_id_type=MESH,
                    )
                )
        arrivals[-offset] = sends[offset]
    for offset in (1, -1, 0):
        where_present(offset, lambda: [copy.start() for copy in sends[offset]])

    loads[5].wait()
    for slot in range(8):
        for f in range(2):
            for edge in range(2):
                feature_send[edge, slot, f] = feature_ref[cache_rows[slot], f, edge]
    edges = {
        offset: pltpu.make_async_remote_copy(
            src_ref=feature_send.at[edge],
            dst_ref=cached_ref.at[:, :, at : at + WIDTH, :],
            send_sem=feature_ssem.at[edge],
            recv_sem=feature_rsem.at[edge],
            device_id=peer(offset, 0),
            device_id_type=MESH,
        )
        for edge, offset, at in ((1, 1, 0), (0, -1, WINDOW - WIDTH))
    }
    for offset in (1, -1):
        where_present(offset, lambda: edges[offset].start())
    for slot in range(8):
        for f in range(2):
            for y in range(ROWS):
                at = (1 + y) * WIDTH
                cached_ref[slot, f, at : at + WIDTH, :] = feature_send[y, slot, f]
    loads[6].wait()

    def combine(i, carry):
        at = pl.multiple_of(i * 16, 16)
        taps = [
            [out_weight_ref[b, c, pl.ds(at, 16), :].astype(F32) for c in range(3)] for b in range(3)
        ]
        rows = (
            (taps[0], [u + v for u, v in zip(taps[1], taps[2])]),
            ([u + v for u, v in zip(taps[0], taps[1])], taps[2]),
        )
        for py in range(2):
            for ty in range(2):
                line = rows[py][ty]
                columns = ((line[0], line[1] + line[2]), (line[0] + line[1], line[2]))
                for px in range(2):
                    for tx in range(2):
                        k = (2 * ty + tx) * MIDDLE_CHANNELS
                        phase_ref[2 * py + px, pl.ds(at, 16), k : k + MIDDLE_CHANNELS] = columns[px][
                            tx
                        ].astype(BF16)
        return carry

    lax.fori_loop(0, OUTPUT_CHANNELS // 16, combine, 0)
    for offset in (1, -1, 0):
        where_present(offset, lambda: [copy.wait_recv() for copy in arrivals[offset]])

    lane = lax.broadcasted_iota(jnp.int32, (LATENT_CHANNELS, 128), 1)
    column = lane % WIDTH

    def turned(value, by):
        return pltpu.roll(value, by % 128, 1)

    def gather_patches(slot, carry):
        count = count_ref[slot]
        turn = lax.rem(group - slot // 2 + 4, 4)
        k = slot % 2
        for pair in range(3):
            blocks = []
            for place in range(3):
                if pair == 0:
                    block = cache_recv[place, slot].astype(F32)
                else:
                    block = latent_recv[place, turn, k, pair - 1].astype(F32)
                    frame = 2 * (pair - 1) + lane // 64
                    block = jnp.where(frame < count, block, 0.0)
                if place == 0:
                    block = jnp.where(tile > 0, block, 0.0)
                if place == 2:
                    block = jnp.where(tile < tiles - 1, block, 0.0)
                blocks.append(block)
            up, own, down = blocks
            own_half = turned(own, 64)
            windows = (
                (
                    jnp.where(lane < 64, up, own_half),
                    jnp.where(
                        lane < 32,
                        turned(up, -32),
                        jnp.where(lane < 96, turned(own, 32), turned(down, -32)),
                    ),
                    jnp.where(lane < 64, own, turned(down, 64)),
                ),
                (
                    jnp.where(lane < 64, turned(up, 64), own),
                    jnp.where(
                        lane < 32,
                        turned(up, 32),
                        jnp.where(lane < 96, turned(own, -32), turned(down, 32)),
                    ),
                    jnp.where(lane < 64, own_half, down),
                ),
            )
            for half in range(2):
                base = (slot * SEQ + 2 * pair + half) * PATCH
                for b in range(3):
                    window = windows[half][b]
                    shifted = (
                        jnp.where(column == 0, 0.0, turned(window, 1)),
                        window,
                        jnp.where(column == WIDTH - 1, 0.0, turned(window, -1)),
                    )
                    for c in range(3):
                        at = pl.multiple_of(base + (3 * b + c) * 16, 16)
                        patch_ref[pl.ds(at, 16), :] = shifted[c].astype(BF16)
        return carry

    lax.fori_loop(0, 8, gather_patches, 0)
    for offset in (1, -1, 0):
        where_present(offset, lambda: [copy.wait_send() for copy in sends[offset]])
    for offset in (1, -1):
        where_present(offset, lambda: edges[offset].wait_send())
        where_present(-offset, lambda: edges[offset].wait_recv())

    for edge, gone in ((0, tile == 0), (WINDOW - WIDTH, tile == tiles - 1)):

        @pl.when(gone)
        def _():
            cached_ref[:, :, edge : edge + WIDTH, :] = jnp.zeros(
                (8, 2, WIDTH, MIDDLE_CHANNELS), BF16
            )


def decode_kernel(
    dest_ref,
    valid_ref,
    cached_ref,
    patch_ref,
    in_weight_ref,
    in_bias_ref,
    gain_ref,
    time_weight_ref,
    time_bias_ref,
    out_weight_ref,
    out_bias_ref,
    out_ref,
    count_ref,
    work_ref,
    seq_ref,
    shift_ref,
    low_ref,
    high_ref,
    stage_ref,
    zero_ref,
    zero_sem,
    stage_sem,
):
    group = lax.axis_index("req")
    tile = lax.axis_index("tile")
    tiles = lax.axis_size("tile")

    total = jnp.int32(0)
    last = jnp.int32(0)
    for source in range(4):
        first, second, seen = pick_two(dest_ref, 4 * source, group)
        for k, local in ((0, first), (1, second)):
            slot = 2 * source + k
            count = jnp.where(seen > k, valid_ref[4 * source + local], 0)
            count_ref[slot] = count
            for f in range(FRAMES):
                work_ref[total] = jnp.int32(slot * FRAMES + f)
                keep = f < count
                last = jnp.where(keep, slot * FRAMES + f, last)
                total = total + keep.astype(jnp.int32)
    for extra in range(2 * GROUP):
        work_ref[total + extra] = last
    steps = (total + GROUP - 1) // GROUP

    zero_ref[...] = jnp.zeros_like(zero_ref)

    def zero_copy(i):
        return pltpu.make_async_copy(
            zero_ref, out_ref.at[i // FRAMES, pl.ds(2 * (i % FRAMES), 2)], zero_sem.at[i]
        )

    @pl.loop(0, 8 * FRAMES)
    def _(i):
        @pl.when((i % FRAMES) >= count_ref[i // FRAMES])
        def _():
            zero_copy(i).start()

    for slot in range(8):

        @pl.when(count_ref[slot] > 0)
        def _():
            seq_ref[slot, 0:2] = cached_ref[slot]

    half_gain = 0.5 * gain_ref[...][None, :]
    in_bias = in_bias_ref[...][None, :]

    def in_conv(step):
        for part in range(GROUP // 2):
            places = []
            pieces = []
            for u in range(2):
                item = work_ref[step * GROUP + 2 * part + u]
                slot, f = item // FRAMES, item % FRAMES
                places.append((slot, f))
                at = pl.multiple_of((slot * SEQ + f) * PATCH, 16)
                pieces.append(patch_ref[pl.ds(at, 3 * PATCH), :])
            inner = (
                lax.dot_general(
                    jnp.concatenate(pieces, axis=1),
                    in_weight_ref[...],
                    (((0,), (0,)), ((), ())),
                    preferred_element_type=F32,
                )
                + in_bias
            )
            scale = lax.rsqrt(jnp.mean(inner * inner, axis=-1, keepdims=True) + EPSILON)
            half = inner * scale * half_gain
            active = (half + half * jnp.tanh(half)).astype(BF16)
            for u, (slot, f) in enumerate(places):
                seq_ref[slot, f + 2] = active[u * WINDOW : (u + 1) * WINDOW]

    pixel = lax.broadcasted_iota(jnp.int32, (WINDOW, 2 * MIDDLE_CHANNELS), 0)
    inside = ((pixel >= WIDTH) | (tile > 0)) & ((pixel < WINDOW - WIDTH) | (tile < tiles - 1))
    pixel_column = pixel % WIDTH

    def stage_copy(buffer, u, item):
        return pltpu.make_async_copy(
            stage_ref.at[buffer, u],
            out_ref.at[item // FRAMES, pl.ds(2 * (item % FRAMES), 2)],
            stage_sem.at[buffer, u],
        )

    @pl.when(steps > 0)
    def _():
        in_conv(0)

    @pl.loop(0, steps)
    def _(step):
        buffer = step % 2
        items = [work_ref[step * GROUP + u] for u in range(GROUP)]
        rows = []
        for u in range(GROUP):
            slot, f = items[u] // FRAMES, items[u] % FRAMES
            rows.append(jnp.concatenate([seq_ref[slot, f + a] for a in range(3)], axis=1))
        doubled = (
            jnp.dot(
                jnp.concatenate(rows, axis=0), time_weight_ref[...], preferred_element_type=F32
            )
            + time_bias_ref[...][None, :]
        )
        in_conv(step + 1)
        for u in range(GROUP):
            own = doubled[u * WINDOW : (u + 1) * WINDOW].astype(BF16).astype(F32)
            own = jnp.where(inside, own, 0.0)
            before = jnp.where(pixel_column == 0, 0.0, pltpu.roll(own, 1, 0))
            after = jnp.where(pixel_column == WIDTH - 1, 0.0, pltpu.roll(own, WINDOW - 1, 0))
            for c, value in enumerate((before, own, after)):
                value = value.astype(BF16)
                for h in range(2):
                    shift_ref[c, 2 * u + h] = value[:, h * MIDDLE_CHANNELS : (h + 1) * MIDDLE_CHANNELS]

        for py in range(2):
            for px in range(2):
                taps = []
                for ty in range(2):
                    for tx in range(2):
                        a = (py + ty) * WIDTH
                        taps.append(
                            shift_ref[px + tx, :, a : a + ROWS * WIDTH, :].reshape(
                                2 * GROUP * ROWS * WIDTH, MIDDLE_CHANNELS
                            )
                        )
                result = (
                    lax.dot_general(
                        jnp.concatenate(taps, axis=1),
                        out_weight_ref[2 * py + px],
                        (((1,), (1,)), ((), ())),
                        preferred_element_type=F32,
                    )
                    + out_bias_ref[...][None, :]
                )
                for q in range(2 * GROUP):
                    for y in range(ROWS):
                        at = (q * ROWS + y) * WIDTH
                        spread = pl.ds(px, WIDTH, stride=2)
                        part = result[at : at + WIDTH]
                        low_ref[q, 2 * y + py, spread, :] = part[:, :128]
                        high_ref[q, 2 * y + py, spread, 0 : OUTPUT_CHANNELS - 128] = part[:, 128:]

        @pl.when(step >= 2)
        def _():
            for u in range(GROUP):
                stage_copy(buffer, u, 0).wait()

        for u in range(GROUP):
            stage_ref[buffer, u, :, :, :, 0:128] = low_ref[2 * u : 2 * u + 2].astype(BF16)
            stage_ref[buffer, u, :, :, :, 128:OUTPUT_CHANNELS] = high_ref[
                2 * u : 2 * u + 2, :, :, 0 : OUTPUT_CHANNELS - 128
            ].astype(BF16)
            if u == 0:
                stage_copy(buffer, u, items[u]).start()
            else:

                @pl.when(step * GROUP + u < total)
                def _():
                    stage_copy(buffer, u, items[u]).start()

    for back in range(2, 0, -1):

        @pl.when(steps >= back)
        def _():
            step = steps - back
            for u in range(GROUP):

                @pl.when(step * GROUP + u < total)
                def _():
                    stage_copy(step % 2, u, 0).wait()

    @pl.loop(0, 8 * FRAMES)
    def _(i):
        @pl.when((i % FRAMES) >= count_ref[i // FRAMES])
        def _():
            zero_copy(i).wait()


def per_device(
    latent,
    destination,
    valid_frames,
    cache_slot,
    latent_cache,
    feature_cache,
    in_weight,
    in_bias,
    norm_gain,
    time_weight,
    time_bias,
    out_weight,
    out_bias,
):
    groups = lax.axis_size("req")
    tiles = lax.axis_size("tile")
    target = destination[:, 0]
    smem = pl.BlockSpec(memory_space=pltpu.SMEM)
    vmem = pl.BlockSpec(memory_space=pltpu.VMEM)
    hbm = pl.BlockSpec(memory_space=pltpu.HBM)
    shape = jax.ShapeDtypeStruct
    dma = pltpu.SemaphoreType.DMA
    slots = 8

    in_hbm = functools.partial(pltpu.with_memory_space_constraint, memory_space=pltpu.HBM)

    cached, patches, phase_weight = pl.pallas_call(
        functools.partial(exchange_kernel, groups, tiles),
        out_shape=(
            pltpu.VMEM((slots, 2, WINDOW, MIDDLE_CHANNELS), BF16),
            pltpu.VMEM((slots * SEQ * PATCH, WINDOW), BF16),
            pltpu.VMEM((4, OUTPUT_CHANNELS, 4 * MIDDLE_CHANNELS), BF16),
        ),
        in_specs=[hbm] * 7,
        out_specs=(vmem, vmem, vmem),
        scratch_shapes=[
            pltpu.SMEM((16,), jnp.int32),
            pltpu.SMEM((16,), jnp.int32),
            pltpu.SMEM((16,), jnp.int32),
            pltpu.VMEM((4, FRAMES, ROWS, LATENT_CHANNELS, WIDTH), BF16),
            pltpu.VMEM((16, 2, ROWS, LATENT_CHANNELS, WIDTH), BF16),
            pltpu.VMEM((16, 2, ROWS, WIDTH, MIDDLE_CHANNELS), BF16),
            pltpu.VMEM((3, 3, OUTPUT_CHANNELS, MIDDLE_CHANNELS), BF16),
            pltpu.VMEM((4, CAPACITY, 2, LATENT_CHANNELS, 128), BF16),
            pltpu.VMEM((slots, LATENT_CHANNELS, 128), BF16),
            pltpu.VMEM((2, slots, 2, WIDTH, MIDDLE_CHANNELS), BF16),
            pltpu.VMEM((3, 4, CAPACITY, 2, LATENT_CHANNELS, 128), BF16),
            pltpu.VMEM((3, slots, LATENT_CHANNELS, 128), BF16),
            pltpu.SMEM((slots,), jnp.int32),
            dma((3, 4)),
            dma((3, 4)),
            dma((3,)),
            dma((3,)),
            dma((2,)),
            dma((2,)),
            dma((7,)),
        ],
        compiler_params=pltpu.CompilerParams(
            collective_id=0, has_side_effects=True, vmem_limit_bytes=VMEM_LIMIT
        ),
        name="exchange",
    )(
        in_hbm(target),
        in_hbm(valid_frames),
        in_hbm(cache_slot),
        in_hbm(jnp.transpose(latent, (0, 1, 2, 4, 3))),
        in_hbm(jnp.transpose(latent_cache, (0, 1, 2, 4, 3))),
        in_hbm(feature_cache),
        in_hbm(jnp.transpose(out_weight, (0, 1, 3, 2))),
    )

    return pl.pallas_call(
        decode_kernel,
        out_shape=shape((slots, 2 * FRAMES, 2 * ROWS, 2 * WIDTH, OUTPUT_CHANNELS), BF16),
        in_specs=[smem, smem] + [vmem] * 9,
        out_specs=hbm,
        scratch_shapes=[
            pltpu.SMEM((slots,), jnp.int32),
            pltpu.SMEM((slots * FRAMES + 2 * GROUP,), jnp.int32),
            pltpu.VMEM((slots, SEQ, WINDOW, MIDDLE_CHANNELS), BF16),
            pltpu.VMEM((3, 2 * GROUP, WINDOW, MIDDLE_CHANNELS), BF16),
            pltpu.VMEM((2 * GROUP, 2 * ROWS, 2 * WIDTH, 128), F32),
            pltpu.VMEM((2 * GROUP, 2 * ROWS, 2 * WIDTH, 128), F32),
            pltpu.VMEM((2, GROUP, 2, 2 * ROWS, 2 * WIDTH, OUTPUT_CHANNELS), BF16),
            pltpu.VMEM((2, 2 * ROWS, 2 * WIDTH, OUTPUT_CHANNELS), BF16),
            dma((slots * FRAMES,)),
            dma((2, GROUP)),
        ],
        compiler_params=pltpu.CompilerParams(vmem_limit_bytes=VMEM_LIMIT),
        name="decode",
    )(
        target,
        valid_frames,
        cached,
        patches,
        in_weight.reshape(27 * LATENT_CHANNELS, MIDDLE_CHANNELS),
        in_bias,
        norm_gain,
        time_weight.reshape(3 * MIDDLE_CHANNELS, 2 * MIDDLE_CHANNELS),
        time_bias,
        phase_weight,
        out_bias,
    )


def solution(mesh):
    placed = (
        P("req", None, "tile", None, None),
        P(),
        P(),
        P(),
        P("req", None, "tile", None, None),
        P("req", None, "tile", None, None),
        P(),
        P(),
        P(),
        P(),
        P(),
        P(),
        P(),
    )
    return jax.shard_map(
        per_device,
        mesh=mesh,
        in_specs=placed,
        out_specs=P("req", None, "tile", None, None),
        check_vma=False,
    )
```

```python
import functools

import jax
import jax.numpy as jnp
from jax import lax
from jax.experimental import pallas as pl
from jax.experimental.pallas import tpu as pltpu
from jax.sharding import PartitionSpec as P

LATENT_CHANNELS = 16
MIDDLE_CHANNELS = 384
OUTPUT_CHANNELS = 192
FRAMES = 4
CAPACITY = 2
EPSILON = 1e-06

ROWS = 2
WIDTH = 32
WINDOW = (ROWS + 2) * WIDTH
PATCH = 9 * LATENT_CHANNELS
SEQ = FRAMES + 2
GROUP = 4
VMEM_LIMIT = 28 * 2**20

MESH = pl.DeviceIdType.MESH
BF16 = jnp.bfloat16
F32 = jnp.float32


def pick_two(dest_ref, start, target):
    seen = jnp.int32(0)
    first = jnp.int32(0)
    second = jnp.int32(0)
    for j in range(4):
        hit = dest_ref[start + j] == target
        first = jnp.where(hit & (seen == 0), j, first)
        second = jnp.where(hit & (seen == 1), j, second)
        seen = seen + hit.astype(jnp.int32)
    return first, second, seen


def lane_join(pieces):
    return jnp.concatenate([p.astype(F32) for p in pieces], axis=-1).astype(BF16)


def exchange_kernel(
    groups,
    tiles,
    dest_hbm,
    valid_hbm,
    cache_slot_hbm,
    latent_hbm,
    latent_cache_hbm,
    feature_hbm,
    out_weight_hbm,
    cached_ref,
    patch_ref,
    phase_ref,
    dest_ref,
    valid_ref,
    cache_slot_ref,
    latent_ref,
    latent_cache_ref,
    feature_ref,
    out_weight_ref,
    packed_ref,
    feature_send,
    near_ref,
    far_ref,
    count_ref,
    near_ssem,
    near_rsem,
    far_ssem,
    far_rsem,
    feature_ssem,
    feature_rsem,
    load_sem,
):
    group = lax.axis_index("req")
    tile = lax.axis_index("tile")
    loads = [
        pltpu.make_async_copy(source, target, load_sem.at[i])
        for i, (source, target) in enumerate(
            (
                (dest_hbm, dest_ref),
                (cache_slot_hbm, cache_slot_ref),
                (valid_hbm, valid_ref),
                (latent_hbm, latent_ref),
                (latent_cache_hbm, latent_cache_ref),
                (feature_hbm, feature_ref),
                (out_weight_hbm, out_weight_ref),
            )
        )
    ]

    def peer(offset, turn):
        return (lax.rem(group + turn, groups), lax.rem(tile + offset + tiles, tiles))

    present = {-1: tile > 0, 0: None, 1: tile < tiles - 1}

    def where_present(offset, act):
        def run():
            act()

        if offset == 0:
            run()
        else:
            pl.when(present[offset])(run)

    barrier = pltpu.get_barrier_semaphore()
    for offset in (1, -1):
        where_present(
            offset,
            lambda: pl.semaphore_signal(
                barrier, inc=1, device_id=peer(offset, 0), device_id_type=MESH
            ),
        )
    for turn in range(1, 4):
        pl.semaphore_signal(barrier, inc=1, device_id=peer(0, turn), device_id_type=MESH)
    for load in loads:
        load.start()

    for load in loads[:3]:
        load.wait()

    cache_rows = []
    for source in range(4):
        first, second, seen = pick_two(dest_ref, 4 * source, group)
        for k, local in ((0, first), (1, second)):
            r = 4 * source + local
            cache_rows.append(cache_slot_ref[r])
            count_ref[2 * source + k] = jnp.where(seen > k, valid_ref[r], 0)
    picks = [
        pick_two(dest_ref, 4 * group, lax.rem(group + turn, groups))[:2] for turn in range(4)
    ]

    loads[3].wait()
    for turn in range(4):
        for k in range(CAPACITY):
            for pair in range(2):
                block = lane_join(
                    [latent_ref[picks[turn][k], 2 * pair + f, y] for f in range(2) for y in range(2)]
                )
                at = 4 * turn + 2 * k + pair
                packed_ref[at] = block
                near_ref[1, at] = block
    loads[4].wait()
    for slot in range(8):
        block = lane_join(
            [latent_cache_ref[cache_rows[slot], f, y] for f in range(2) for y in range(2)]
        )
        packed_ref[16 + slot] = block
        near_ref[1, 16 + slot] = block

    sides = (tile > 0).astype(jnp.int32) + (tile < tiles - 1).astype(jnp.int32)
    pl.semaphore_wait(barrier, 3 + sides)
    near = {
        offset: pltpu.make_async_remote_copy(
            src_ref=packed_ref,
            dst_ref=near_ref.at[1 - offset],
            send_sem=near_ssem.at[1 - offset],
            recv_sem=near_rsem.at[1 - offset],
            device_id=peer(offset, 0),
            device_id_type=MESH,
        )
        for offset in (1, -1)
    }
    for offset in (1, -1):
        where_present(offset, lambda: near[offset].start())

    loads[5].wait()
    for slot in range(8):
        for f in range(2):
            for edge in range(2):
                feature_send[edge, slot, f] = feature_ref[cache_rows[slot], f, edge]
    edges = {
        offset: pltpu.make_async_remote_copy(
            src_ref=feature_send.at[edge],
            dst_ref=cached_ref.at[:, :, at : at + WIDTH, :],
            send_sem=feature_ssem.at[edge],
            recv_sem=feature_rsem.at[edge],
            device_id=peer(offset, 0),
            device_id_type=MESH,
        )
        for edge, offset, at in ((1, 1, 0), (0, -1, WINDOW - WIDTH))
    }
    for offset in (1, -1):
        where_present(offset, lambda: edges[offset].start())
    for slot in range(8):
        for f in range(2):
            for y in range(ROWS):
                at = (1 + y) * WIDTH
                cached_ref[slot, f, at : at + WIDTH, :] = feature_send[y, slot, f]
    for place, gone in ((0, tile == 0), (2, tile == tiles - 1)):

        @pl.when(gone)
        def _():
            near_ref[place] = jnp.zeros((24, LATENT_CHANNELS, 128), BF16)

    for offset in (1, -1):
        where_present(-offset, lambda: near[offset].wait_recv())
    far = []
    for turn in (2, 1, 3):
        part = pl.ds(4 * turn, 4)
        far.append(
            pltpu.make_async_remote_copy(
                src_ref=near_ref.at[:, part],
                dst_ref=far_ref.at[:, part],
                send_sem=far_ssem.at[turn],
                recv_sem=far_rsem.at[turn],
                device_id=peer(0, turn),
                device_id_type=MESH,
            )
        )
    for copy in far:
        copy.start()
    far_ref[:, 0:4] = near_ref[:, 0:4]
    loads[6].wait()

    def combine(i, carry):
        at = pl.multiple_of(i * 16, 16)
        taps = [
            [out_weight_ref[b, c, pl.ds(at, 16), :].astype(F32) for c in range(3)] for b in range(3)
        ]
        rows = (
            (taps[0], [u + v for u, v in zip(taps[1], taps[2])]),
            ([u + v for u, v in zip(taps[0], taps[1])], taps[2]),
        )
        for py in range(2):
            for ty in range(2):
                left, middle, right = rows[py][ty]
                k = ty * MIDDLE_CHANNELS
                for part, value in enumerate((left, left + middle + right, right)):
                    phase_ref[3 * py + part, pl.ds(at, 16), k : k + MIDDLE_CHANNELS] = value.astype(
                        BF16
                    )
        return carry

    lax.fori_loop(0, OUTPUT_CHANNELS // 16, combine, 0)
    for copy in far:
        copy.wait_recv()

    lane = lax.broadcasted_iota(jnp.int32, (LATENT_CHANNELS, 128), 1)
    column = lane % WIDTH

    def turned(value, by):
        return pltpu.roll(value, by % 128, 1)

    def gather_patches(slot, carry):
        count = count_ref[slot]
        turn = lax.rem(group - slot // 2 + 4, 4)
        k = slot % 2
        for pair in range(3):
            blocks = []
            for place in range(3):
                if pair == 0:
                    block = near_ref[place, 16 + slot].astype(F32)
                else:
                    block = far_ref[place, 4 * turn + 2 * k + pair - 1].astype(F32)
                    frame = 2 * (pair - 1) + lane // 64
                    block = jnp.where(frame < count, block, 0.0)
                if place == 0:
                    block = jnp.where(tile > 0, block, 0.0)
                if place == 2:
                    block = jnp.where(tile < tiles - 1, block, 0.0)
                blocks.append(block)
            up, own, down = blocks
            own_half = turned(own, 64)
            windows = (
                (
                    jnp.where(lane < 64, up, own_half),
                    jnp.where(
                        lane < 32,
                        turned(up, -32),
                        jnp.where(lane < 96, turned(own, 32), turned(down, -32)),
                    ),
                    jnp.where(lane < 64, own, turned(down, 64)),
                ),
                (
                    jnp.where(lane < 64, turned(up, 64), own),
                    jnp.where(
                        lane < 32,
                        turned(up, 32),
                        jnp.where(lane < 96, turned(own, -32), turned(down, 32)),
                    ),
                    jnp.where(lane < 64, own_half, down),
                ),
            )
            for half in range(2):
                base = (slot * SEQ + 2 * pair + half) * PATCH
                for b in range(3):
                    window = windows[half][b]
                    shifted = (
                        jnp.where(column == 0, 0.0, turned(window, 1)),
                        window,
                        jnp.where(column == WIDTH - 1, 0.0, turned(window, -1)),
                    )
                    for c in range(3):
                        at = pl.multiple_of(base + (3 * b + c) * 16, 16)
                        patch_ref[pl.ds(at, 16), :] = shifted[c].astype(BF16)
        return carry

    lax.fori_loop(0, 8, gather_patches, 0, unroll=2)
    for copy in far:
        copy.wait_send()
    for offset in (1, -1):
        where_present(offset, lambda: near[offset].wait_send())
        where_present(offset, lambda: edges[offset].wait_send())
        where_present(-offset, lambda: edges[offset].wait_recv())

    for edge, gone in ((0, tile == 0), (WINDOW - WIDTH, tile == tiles - 1)):

        @pl.when(gone)
        def _():
            cached_ref[:, :, edge : edge + WIDTH, :] = jnp.zeros(
                (8, 2, WIDTH, MIDDLE_CHANNELS), BF16
            )


def decode_kernel(
    dest_ref,
    valid_ref,
    cached_ref,
    patch_ref,
    in_weight_ref,
    in_bias_ref,
    gain_ref,
    time_weight_ref,
    time_bias_ref,
    out_weight_ref,
    out_bias_ref,
    out_ref,
    count_ref,
    work_ref,
    seq_ref,
    shift_ref,
    low_ref,
    high_ref,
    stage_ref,
    zero_ref,
    zero_sem,
    stage_sem,
):
    group = lax.axis_index("req")
    tile = lax.axis_index("tile")
    tiles = lax.axis_size("tile")

    total = jnp.int32(0)
    last = jnp.int32(0)
    for source in range(4):
        first, second, seen = pick_two(dest_ref, 4 * source, group)
        for k, local in ((0, first), (1, second)):
            slot = 2 * source + k
            count = jnp.where(seen > k, valid_ref[4 * source + local], 0)
            count_ref[slot] = count
            for f in range(FRAMES):
                work_ref[total] = jnp.int32(slot * FRAMES + f)
                keep = f < count
                last = jnp.where(keep, slot * FRAMES + f, last)
                total = total + keep.astype(jnp.int32)
    for extra in range(2 * GROUP):
        work_ref[total + extra] = last
    steps = (total + GROUP - 1) // GROUP

    zero_ref[...] = jnp.zeros_like(zero_ref)

    def each_zero(act):
        @pl.loop(0, 8)
        def _(slot):
            count = count_ref[slot]
            missing = FRAMES - count
            for size in (1, 2, 4):
                at = 2 * jnp.where(size == 1, count, FRAMES - size)

                @pl.when((missing & size) > 0)
                def _():
                    act(
                        pltpu.make_async_copy(
                            zero_ref.at[pl.ds(0, 2 * size)],
                            out_ref.at[slot, pl.ds(at, 2 * size)],
                            zero_sem.at[slot, size // 2],
                        )
                    )

    each_zero(lambda copy: copy.start())

    for slot in range(8):

        @pl.when(count_ref[slot] > 0)
        def _():
            seq_ref[slot, 0:2] = cached_ref[slot]

    half_gain = 0.5 * gain_ref[...][None, :]
    in_bias = in_bias_ref[...][None, :]

    def in_conv(step):
        for part in range(GROUP // 2):
            places = []
            pieces = []
            for u in range(2):
                item = work_ref[step * GROUP + 2 * part + u]
                slot, f = item // FRAMES, item % FRAMES
                places.append((slot, f))
                at = pl.multiple_of((slot * SEQ + f) * PATCH, 16)
                pieces.append(patch_ref[pl.ds(at, 3 * PATCH), :])
            inner = (
                lax.dot_general(
                    jnp.concatenate(pieces, axis=1),
                    in_weight_ref[...],
                    (((0,), (0,)), ((), ())),
                    preferred_element_type=F32,
                )
                + in_bias
            )
            scale = lax.rsqrt(jnp.mean(inner * inner, axis=-1, keepdims=True) + EPSILON)
            half = inner * scale * half_gain
            active = (half + half * jnp.tanh(half)).astype(BF16)
            for u, (slot, f) in enumerate(places):
                seq_ref[slot, f + 2] = active[u * WINDOW : (u + 1) * WINDOW]

    pixel_column = lax.broadcasted_iota(jnp.int32, (WINDOW, 2 * MIDDLE_CHANNELS), 0) % WIDTH
    first_column = pixel_column == 0
    last_column = pixel_column == WIDTH - 1

    def stage_copy(buffer, u, item):
        return pltpu.make_async_copy(
            stage_ref.at[buffer, u],
            out_ref.at[item // FRAMES, pl.ds(2 * (item % FRAMES), 2)],
            stage_sem.at[buffer, u],
        )

    @pl.when(steps > 0)
    def _():
        in_conv(0)

    @pl.loop(0, steps)
    def _(step):
        buffer = step % 2
        items = [work_ref[step * GROUP + u] for u in range(GROUP)]
        rows = []
        for u in range(GROUP):
            slot, f = items[u] // FRAMES, items[u] % FRAMES
            rows.append(jnp.concatenate([seq_ref[slot, f + a] for a in range(3)], axis=1))
        doubled = (
            jnp.dot(
                jnp.concatenate(rows, axis=0), time_weight_ref[...], preferred_element_type=F32
            )
            + time_bias_ref[...][None, :]
        )
        for u in range(GROUP):
            own = doubled[u * WINDOW : (u + 1) * WINDOW]
            own = jnp.concatenate(
                [
                    jnp.where(tile > 0, own[:WIDTH], 0.0),
                    own[WIDTH : WINDOW - WIDTH],
                    jnp.where(tile < tiles - 1, own[WINDOW - WIDTH :], 0.0),
                ],
                axis=0,
            )
            middle = own.astype(BF16)
            before = jnp.where(first_column, 0.0, pltpu.roll(own, 1, 0).astype(BF16))
            after = jnp.where(last_column, 0.0, pltpu.roll(own, WINDOW - 1, 0).astype(BF16))
            for c, value in enumerate((before - middle, middle, after - middle)):
                for h in range(2):
                    shift_ref[c, 2 * u + h] = value[:, h * MIDDLE_CHANNELS : (h + 1) * MIDDLE_CHANNELS]

        in_conv(step + 1)
        for py in range(2):
            products = []
            for part in range(3):
                taps = []
                for ty in range(2):
                    a = (py + ty) * WIDTH
                    taps.append(
                        shift_ref[part, :, a : a + ROWS * WIDTH, :].reshape(
                            2 * GROUP * ROWS * WIDTH, MIDDLE_CHANNELS
                        )
                    )
                products.append(
                    lax.dot_general(
                        jnp.concatenate(taps, axis=1),
                        out_weight_ref[3 * py + part],
                        (((1,), (1,)), ((), ())),
                        preferred_element_type=F32,
                    )
                )
            shared = products[1] + out_bias_ref[...][None, :]
            for px in range(2):
                result = shared + products[2 * px]
                for q in range(2 * GROUP):
                    for y in range(ROWS):
                        at = (q * ROWS + y) * WIDTH
                        spread = pl.ds(px, WIDTH, stride=2)
                        part = result[at : at + WIDTH]
                        low_ref[q, 2 * y + py, spread, :] = part[:, :128]
                        high_ref[q, 2 * y + py, spread, 0 : OUTPUT_CHANNELS - 128] = part[:, 128:]

        @pl.when(step >= 2)
        def _():
            for u in range(GROUP):
                stage_copy(buffer, u, 0).wait()

        for u in range(GROUP):
            stage_ref[buffer, u, :, :, :, 0:128] = low_ref[2 * u : 2 * u + 2].astype(BF16)
            stage_ref[buffer, u, :, :, :, 128:OUTPUT_CHANNELS] = high_ref[
                2 * u : 2 * u + 2, :, :, 0 : OUTPUT_CHANNELS - 128
            ].astype(BF16)
            if u == 0:
                stage_copy(buffer, u, items[u]).start()
            else:

                @pl.when(step * GROUP + u < total)
                def _():
                    stage_copy(buffer, u, items[u]).start()

    for back in range(2, 0, -1):

        @pl.when(steps >= back)
        def _():
            step = steps - back
            for u in range(GROUP):

                @pl.when(step * GROUP + u < total)
                def _():
                    stage_copy(step % 2, u, 0).wait()

    each_zero(lambda copy: copy.wait())


def per_device(
    latent,
    destination,
    valid_frames,
    cache_slot,
    latent_cache,
    feature_cache,
    in_weight,
    in_bias,
    norm_gain,
    time_weight,
    time_bias,
    out_weight,
    out_bias,
):
    groups = lax.axis_size("req")
    tiles = lax.axis_size("tile")
    target = destination[:, 0]
    smem = pl.BlockSpec(memory_space=pltpu.SMEM)
    vmem = pl.BlockSpec(memory_space=pltpu.VMEM)
    hbm = pl.BlockSpec(memory_space=pltpu.HBM)
    shape = jax.ShapeDtypeStruct
    dma = pltpu.SemaphoreType.DMA
    slots = 8

    in_hbm = functools.partial(pltpu.with_memory_space_constraint, memory_space=pltpu.HBM)

    cached, patches, phase_weight = pl.pallas_call(
        functools.partial(exchange_kernel, groups, tiles),
        out_shape=(
            pltpu.VMEM((slots, 2, WINDOW, MIDDLE_CHANNELS), BF16),
            pltpu.VMEM((slots * SEQ * PATCH, WINDOW), BF16),
            pltpu.VMEM((6, OUTPUT_CHANNELS, 2 * MIDDLE_CHANNELS), BF16),
        ),
        in_specs=[hbm] * 7,
        out_specs=(vmem, vmem, vmem),
        scratch_shapes=[
            pltpu.SMEM((16,), jnp.int32),
            pltpu.SMEM((16,), jnp.int32),
            pltpu.SMEM((16,), jnp.int32),
            pltpu.VMEM((4, FRAMES, ROWS, LATENT_CHANNELS, WIDTH), BF16),
            pltpu.VMEM((16, 2, ROWS, LATENT_CHANNELS, WIDTH), BF16),
            pltpu.VMEM((16, 2, ROWS, WIDTH, MIDDLE_CHANNELS), BF16),
            pltpu.VMEM((3, 3, OUTPUT_CHANNELS, MIDDLE_CHANNELS), BF16),
            pltpu.VMEM((24, LATENT_CHANNELS, 128), BF16),
            pltpu.VMEM((2, slots, 2, WIDTH, MIDDLE_CHANNELS), BF16),
            pltpu.VMEM((3, 24, LATENT_CHANNELS, 128), BF16),
            pltpu.VMEM((3, 16, LATENT_CHANNELS, 128), BF16),
            pltpu.SMEM((slots,), jnp.int32),
            dma((3,)),
            dma((3,)),
            dma((4,)),
            dma((4,)),
            dma((2,)),
            dma((2,)),
            dma((7,)),
        ],
        compiler_params=pltpu.CompilerParams(
            collective_id=0, has_side_effects=True, vmem_limit_bytes=VMEM_LIMIT
        ),
        name="exchange",
    )(
        in_hbm(target),
        in_hbm(valid_frames),
        in_hbm(cache_slot),
        in_hbm(jnp.transpose(latent, (0, 1, 2, 4, 3))),
        in_hbm(jnp.transpose(latent_cache, (0, 1, 2, 4, 3))),
        in_hbm(feature_cache),
        in_hbm(jnp.transpose(out_weight, (0, 1, 3, 2))),
    )

    return pl.pallas_call(
        decode_kernel,
        out_shape=shape((slots, 2 * FRAMES, 2 * ROWS, 2 * WIDTH, OUTPUT_CHANNELS), BF16),
        in_specs=[smem, smem] + [vmem] * 9,
        out_specs=hbm,
        scratch_shapes=[
            pltpu.SMEM((slots,), jnp.int32),
            pltpu.SMEM((slots * FRAMES + 2 * GROUP,), jnp.int32),
            pltpu.VMEM((slots, SEQ, WINDOW, MIDDLE_CHANNELS), BF16),
            pltpu.VMEM((3, 2 * GROUP, WINDOW, MIDDLE_CHANNELS), BF16),
            pltpu.VMEM((2 * GROUP, 2 * ROWS, 2 * WIDTH, 128), F32),
            pltpu.VMEM((2 * GROUP, 2 * ROWS, 2 * WIDTH, 128), F32),
            pltpu.VMEM((2, GROUP, 2, 2 * ROWS, 2 * WIDTH, OUTPUT_CHANNELS), BF16),
            pltpu.VMEM((2 * FRAMES, 2 * ROWS, 2 * WIDTH, OUTPUT_CHANNELS), BF16),
            dma((slots, 3)),
            dma((2, GROUP)),
        ],
        compiler_params=pltpu.CompilerParams(vmem_limit_bytes=VMEM_LIMIT),
        name="decode",
    )(
        target,
        valid_frames,
        cached,
        patches,
        in_weight.reshape(27 * LATENT_CHANNELS, MIDDLE_CHANNELS),
        in_bias,
        norm_gain,
        time_weight.reshape(3 * MIDDLE_CHANNELS, 2 * MIDDLE_CHANNELS),
        time_bias,
        phase_weight,
        out_bias,
    )


def solution(mesh):
    placed = (
        P("req", None, "tile", None, None),
        P(),
        P(),
        P(),
        P("req", None, "tile", None, None),
        P("req", None, "tile", None, None),
        P(),
        P(),
        P(),
        P(),
        P(),
        P(),
        P(),
    )
    return jax.shard_map(
        per_device,
        mesh=mesh,
        in_specs=placed,
        out_specs=P("req", None, "tile", None, None),
        check_vma=False,
    )
```

```python
import functools

import jax
import jax.numpy as jnp
from jax import lax
from jax.experimental import pallas as pl
from jax.experimental.pallas import tpu as pltpu
from jax.sharding import PartitionSpec as P

LATENT_CHANNELS = 16
MIDDLE_CHANNELS = 384
OUTPUT_CHANNELS = 192
FRAMES = 4
CAPACITY = 2
EPSILON = 1e-06

ROWS = 2
WIDTH = 32
WINDOW = (ROWS + 2) * WIDTH
PATCH = 9 * LATENT_CHANNELS
SEQ = FRAMES + 2
GROUP = 4
VMEM_LIMIT = 28 * 2**20

MESH = pl.DeviceIdType.MESH
BF16 = jnp.bfloat16
F32 = jnp.float32


def pick_two(dest_ref, start, target):
    seen = jnp.int32(0)
    first = jnp.int32(0)
    second = jnp.int32(0)
    for j in range(4):
        hit = dest_ref[start + j] == target
        first = jnp.where(hit & (seen == 0), j, first)
        second = jnp.where(hit & (seen == 1), j, second)
        seen = seen + hit.astype(jnp.int32)
    return first, second, seen


def lane_join(pieces):
    return jnp.concatenate([p.astype(F32) for p in pieces], axis=-1).astype(BF16)


def exchange_kernel(
    groups,
    tiles,
    dest_hbm,
    valid_hbm,
    cache_slot_hbm,
    latent_hbm,
    latent_cache_hbm,
    feature_hbm,
    out_weight_hbm,
    cached_ref,
    patch_ref,
    phase_ref,
    dest_ref,
    valid_ref,
    cache_slot_ref,
    latent_ref,
    latent_cache_ref,
    feature_ref,
    out_weight_ref,
    packed_ref,
    feature_send,
    near_ref,
    far_ref,
    count_ref,
    near_ssem,
    near_rsem,
    far_ssem,
    far_rsem,
    feature_ssem,
    feature_rsem,
    load_sem,
):
    group = lax.axis_index("req")
    tile = lax.axis_index("tile")
    loads = [
        pltpu.make_async_copy(source, target, load_sem.at[i])
        for i, (source, target) in enumerate(
            (
                (dest_hbm, dest_ref),
                (cache_slot_hbm, cache_slot_ref),
                (valid_hbm, valid_ref),
                (latent_hbm, latent_ref),
                (latent_cache_hbm, latent_cache_ref),
                (feature_hbm, feature_ref),
                (out_weight_hbm, out_weight_ref),
            )
        )
    ]

    def peer(offset, turn):
        return (lax.rem(group + turn, groups), lax.rem(tile + offset + tiles, tiles))

    present = {-1: tile > 0, 0: None, 1: tile < tiles - 1}

    def where_present(offset, act):
        def run():
            act()

        if offset == 0:
            run()
        else:
            pl.when(present[offset])(run)

    barrier = pltpu.get_barrier_semaphore()
    for offset in (1, -1):
        where_present(
            offset,
            lambda: pl.semaphore_signal(
                barrier, inc=1, device_id=peer(offset, 0), device_id_type=MESH
            ),
        )
    for turn in range(1, 4):
        pl.semaphore_signal(barrier, inc=1, device_id=peer(0, turn), device_id_type=MESH)
    for load in loads:
        load.start()

    for load in loads[:3]:
        load.wait()

    cache_rows = []
    for source in range(4):
        first, second, seen = pick_two(dest_ref, 4 * source, group)
        for k, local in ((0, first), (1, second)):
            r = 4 * source + local
            cache_rows.append(cache_slot_ref[r])
            count_ref[2 * source + k] = jnp.where(seen > k, valid_ref[r], 0)
    picks = [
        pick_two(dest_ref, 4 * group, lax.rem(group + turn, groups))[:2] for turn in range(4)
    ]

    loads[3].wait()
    for turn in range(4):
        for k in range(CAPACITY):
            for pair in range(2):
                block = lane_join(
                    [latent_ref[picks[turn][k], 2 * pair + f, y] for f in range(2) for y in range(2)]
                )
                at = 4 * turn + 2 * k + pair
                packed_ref[at] = block
                near_ref[1, at] = block
    loads[4].wait()
    for slot in range(8):
        block = lane_join(
            [latent_cache_ref[cache_rows[slot], f, y] for f in range(2) for y in range(2)]
        )
        packed_ref[16 + slot] = block
        near_ref[1, 16 + slot] = block

    sides = (tile > 0).astype(jnp.int32) + (tile < tiles - 1).astype(jnp.int32)
    pl.semaphore_wait(barrier, 3 + sides)
    near = {
        offset: pltpu.make_async_remote_copy(
            src_ref=packed_ref,
            dst_ref=near_ref.at[1 - offset],
            send_sem=near_ssem.at[1 - offset],
            recv_sem=near_rsem.at[1 - offset],
            device_id=peer(offset, 0),
            device_id_type=MESH,
        )
        for offset in (1, -1)
    }
    for offset in (1, -1):
        where_present(offset, lambda: near[offset].start())

    loads[5].wait()
    for slot in range(8):
        for f in range(2):
            for edge in range(2):
                feature_send[edge, slot, f] = feature_ref[cache_rows[slot], f, edge]
    edges = {
        offset: pltpu.make_async_remote_copy(
            src_ref=feature_send.at[edge],
            dst_ref=cached_ref.at[:, :, at : at + WIDTH, :],
            send_sem=feature_ssem.at[edge],
            recv_sem=feature_rsem.at[edge],
            device_id=peer(offset, 0),
            device_id_type=MESH,
        )
        for edge, offset, at in ((1, 1, 0), (0, -1, WINDOW - WIDTH))
    }
    for offset in (1, -1):
        where_present(offset, lambda: edges[offset].start())
    for slot in range(8):
        for f in range(2):
            for y in range(ROWS):
                at = (1 + y) * WIDTH
                cached_ref[slot, f, at : at + WIDTH, :] = feature_send[y, slot, f]
    for place, gone in ((0, tile == 0), (2, tile == tiles - 1)):

        @pl.when(gone)
        def _():
            near_ref[place] = jnp.zeros((24, LATENT_CHANNELS, 128), BF16)

    for offset in (1, -1):
        where_present(-offset, lambda: near[offset].wait_recv())
    far = []
    for turn in (2, 1, 3):
        part = pl.ds(4 * turn, 4)
        far.append(
            pltpu.make_async_remote_copy(
                src_ref=near_ref.at[:, part],
                dst_ref=far_ref.at[:, part],
                send_sem=far_ssem.at[turn],
                recv_sem=far_rsem.at[turn],
                device_id=peer(0, turn),
                device_id_type=MESH,
            )
        )
    for copy in far:
        copy.start()
    far_ref[:, 0:4] = near_ref[:, 0:4]
    loads[6].wait()

    def combine(i, carry):
        at = pl.multiple_of(i * 16, 16)
        taps = [
            [out_weight_ref[b, c, pl.ds(at, 16), :].astype(F32) for c in range(3)] for b in range(3)
        ]
        rows = (
            (taps[0], [u + v for u, v in zip(taps[1], taps[2])]),
            ([u + v for u, v in zip(taps[0], taps[1])], taps[2]),
        )
        for py in range(2):
            for ty in range(2):
                left, middle, right = rows[py][ty]
                k = ty * MIDDLE_CHANNELS
                for part, value in enumerate((left, left + middle + right, right)):
                    phase_ref[3 * py + part, pl.ds(at, 16), k : k + MIDDLE_CHANNELS] = value.astype(
                        BF16
                    )
        return carry

    lax.fori_loop(0, OUTPUT_CHANNELS // 16, combine, 0)
    for copy in far:
        copy.wait_recv()

    lane = lax.broadcasted_iota(jnp.int32, (LATENT_CHANNELS, 128), 1)
    column = lane % WIDTH

    def turned(value, by):
        return pltpu.roll(value, by % 128, 1)

    def gather_patches(slot, carry):
        count = count_ref[slot]
        turn = lax.rem(group - slot // 2 + 4, 4)
        k = slot % 2
        for pair in range(3):
            blocks = []
            for place in range(3):
                if pair == 0:
                    block = near_ref[place, 16 + slot].astype(F32)
                else:
                    block = far_ref[place, 4 * turn + 2 * k + pair - 1].astype(F32)
                    frame = 2 * (pair - 1) + lane // 64
                    block = jnp.where(frame < count, block, 0.0)
                if place == 0:
                    block = jnp.where(tile > 0, block, 0.0)
                if place == 2:
                    block = jnp.where(tile < tiles - 1, block, 0.0)
                blocks.append(block)
            up, own, down = blocks
            own_half = turned(own, 64)
            windows = (
                (
                    jnp.where(lane < 64, up, own_half),
                    jnp.where(
                        lane < 32,
                        turned(up, -32),
                        jnp.where(lane < 96, turned(own, 32), turned(down, -32)),
                    ),
                    jnp.where(lane < 64, own, turned(down, 64)),
                ),
                (
                    jnp.where(lane < 64, turned(up, 64), own),
                    jnp.where(
                        lane < 32,
                        turned(up, 32),
                        jnp.where(lane < 96, turned(own, -32), turned(down, 32)),
                    ),
                    jnp.where(lane < 64, own_half, down),
                ),
            )
            for half in range(2):
                base = (slot * SEQ + 2 * pair + half) * PATCH
                for b in range(3):
                    window = windows[half][b]
                    shifted = (
                        jnp.where(column == 0, 0.0, turned(window, 1)),
                        window,
                        jnp.where(column == WIDTH - 1, 0.0, turned(window, -1)),
                    )
                    for c in range(3):
                        at = pl.multiple_of(base + (3 * b + c) * 16, 16)
                        patch_ref[pl.ds(at, 16), :] = shifted[c].astype(BF16)
        return carry

    lax.fori_loop(0, 8, gather_patches, 0, unroll=2)
    for copy in far:
        copy.wait_send()
    for offset in (1, -1):
        where_present(offset, lambda: near[offset].wait_send())
        where_present(offset, lambda: edges[offset].wait_send())
        where_present(-offset, lambda: edges[offset].wait_recv())

    for edge, gone in ((0, tile == 0), (WINDOW - WIDTH, tile == tiles - 1)):

        @pl.when(gone)
        def _():
            cached_ref[:, :, edge : edge + WIDTH, :] = jnp.zeros(
                (8, 2, WIDTH, MIDDLE_CHANNELS), BF16
            )


def decode_kernel(
    dest_ref,
    valid_ref,
    cached_ref,
    patch_ref,
    in_weight_ref,
    in_bias_ref,
    gain_ref,
    time_weight_ref,
    time_bias_ref,
    out_weight_ref,
    out_bias_ref,
    out_ref,
    count_ref,
    work_ref,
    seq_ref,
    shift_ref,
    low_ref,
    high_ref,
    stage_ref,
    zero_ref,
    zero_sem,
    stage_sem,
):
    group = lax.axis_index("req")
    tile = lax.axis_index("tile")
    tiles = lax.axis_size("tile")

    total = jnp.int32(0)
    last = jnp.int32(0)
    for source in range(4):
        first, second, seen = pick_two(dest_ref, 4 * source, group)
        for k, local in ((0, first), (1, second)):
            slot = 2 * source + k
            count = jnp.where(seen > k, valid_ref[4 * source + local], 0)
            count_ref[slot] = count
            for f in range(FRAMES):
                work_ref[total] = jnp.int32(slot * FRAMES + f)
                keep = f < count
                last = jnp.where(keep, slot * FRAMES + f, last)
                total = total + keep.astype(jnp.int32)
    for extra in range(2 * GROUP):
        work_ref[total + extra] = last
    steps = (total + 1) // GROUP
    has_tail = total > steps * GROUP

    zero_ref[...] = jnp.zeros_like(zero_ref)

    def each_zero(act):
        @pl.loop(0, 8)
        def _(slot):
            count = count_ref[slot]
            missing = FRAMES - count
            for size in (1, 2, 4):
                at = 2 * jnp.where(size == 1, count, FRAMES - size)

                @pl.when((missing & size) > 0)
                def _():
                    act(
                        pltpu.make_async_copy(
                            zero_ref.at[pl.ds(0, 2 * size)],
                            out_ref.at[slot, pl.ds(at, 2 * size)],
                            zero_sem.at[slot, size // 2],
                        )
                    )

    each_zero(lambda copy: copy.start())

    for slot in range(8):

        @pl.when(count_ref[slot] > 0)
        def _():
            seq_ref[slot, 0:2] = cached_ref[slot]

    half_gain = 0.5 * gain_ref[...][None, :]
    in_bias = in_bias_ref[...][None, :]

    def in_conv(step):
        for part in range(GROUP // 2):
            places = []
            pieces = []
            for u in range(2):
                item = work_ref[step * GROUP + 2 * part + u]
                slot, f = item // FRAMES, item % FRAMES
                places.append((slot, f))
                at = pl.multiple_of((slot * SEQ + f) * PATCH, 16)
                pieces.append(patch_ref[pl.ds(at, 3 * PATCH), :])
            inner = (
                lax.dot_general(
                    jnp.concatenate(pieces, axis=1),
                    in_weight_ref[...],
                    (((0,), (0,)), ((), ())),
                    preferred_element_type=F32,
                )
                + in_bias
            )
            scale = lax.rsqrt(jnp.mean(inner * inner, axis=-1, keepdims=True) + EPSILON)
            half = inner * scale * half_gain
            active = (half + half * jnp.tanh(half)).astype(BF16)
            for u, (slot, f) in enumerate(places):
                seq_ref[slot, f + 2] = active[u * WINDOW : (u + 1) * WINDOW]

    pixel_column = lax.broadcasted_iota(jnp.int32, (WINDOW, 2 * MIDDLE_CHANNELS), 0) % WIDTH
    first_column = pixel_column == 0
    last_column = pixel_column == WIDTH - 1

    def stage_copy(buffer, u, item):
        return pltpu.make_async_copy(
            stage_ref.at[buffer, u],
            out_ref.at[item // FRAMES, pl.ds(2 * (item % FRAMES), 2)],
            stage_sem.at[buffer, u],
        )

    @pl.when(total > 0)
    def _():
        in_conv(0)

    def decode_items(step, size):
        buffer = step % 2
        items = [work_ref[step * GROUP + u] for u in range(size)]
        rows = []
        for u in range(size):
            slot, f = items[u] // FRAMES, items[u] % FRAMES
            rows.append(jnp.concatenate([seq_ref[slot, f + a] for a in range(3)], axis=1))
        doubled = (
            jnp.dot(
                jnp.concatenate(rows, axis=0), time_weight_ref[...], preferred_element_type=F32
            )
            + time_bias_ref[...][None, :]
        )
        for u in range(size):
            own = doubled[u * WINDOW : (u + 1) * WINDOW]
            own = jnp.concatenate(
                [
                    jnp.where(tile > 0, own[:WIDTH], 0.0),
                    own[WIDTH : WINDOW - WIDTH],
                    jnp.where(tile < tiles - 1, own[WINDOW - WIDTH :], 0.0),
                ],
                axis=0,
            )
            middle = own.astype(BF16)
            before = jnp.where(first_column, 0.0, pltpu.roll(own, 1, 0).astype(BF16))
            after = jnp.where(last_column, 0.0, pltpu.roll(own, WINDOW - 1, 0).astype(BF16))
            for c, value in enumerate((before - middle, middle, after - middle)):
                for h in range(2):
                    shift_ref[c, 2 * u + h] = value[:, h * MIDDLE_CHANNELS : (h + 1) * MIDDLE_CHANNELS]

        if size == GROUP:
            in_conv(step + 1)
        for py in range(2):
            products = []
            for part in range(3):
                taps = []
                for ty in range(2):
                    a = (py + ty) * WIDTH
                    taps.append(
                        shift_ref[part, 0 : 2 * size, a : a + ROWS * WIDTH, :].reshape(
                            2 * size * ROWS * WIDTH, MIDDLE_CHANNELS
                        )
                    )
                products.append(
                    lax.dot_general(
                        jnp.concatenate(taps, axis=1),
                        out_weight_ref[3 * py + part],
                        (((1,), (1,)), ((), ())),
                        preferred_element_type=F32,
                    )
                )
            shared = products[1] + out_bias_ref[...][None, :]
            for px in range(2):
                result = shared + products[2 * px]
                for q in range(2 * size):
                    for y in range(ROWS):
                        at = (q * ROWS + y) * WIDTH
                        spread = pl.ds(px, WIDTH, stride=2)
                        part = result[at : at + WIDTH]
                        low_ref[q, 2 * y + py, spread, :] = part[:, :128]
                        high_ref[q, 2 * y + py, spread, 0 : OUTPUT_CHANNELS - 128] = part[:, 128:]

        @pl.when(step >= 2)
        def _():
            for u in range(GROUP):
                stage_copy(buffer, u, 0).wait()

        for u in range(size):
            stage_ref[buffer, u, :, :, :, 0:128] = low_ref[2 * u : 2 * u + 2].astype(BF16)
            stage_ref[buffer, u, :, :, :, 128:OUTPUT_CHANNELS] = high_ref[
                2 * u : 2 * u + 2, :, :, 0 : OUTPUT_CHANNELS - 128
            ].astype(BF16)
            if u == 0:
                stage_copy(buffer, u, items[u]).start()
            else:

                @pl.when(step * GROUP + u < total)
                def _():
                    stage_copy(buffer, u, items[u]).start()

    @pl.loop(0, steps)
    def _(step):
        decode_items(step, GROUP)

    @pl.when(has_tail)
    def _():
        decode_items(steps, GROUP // 2)

    ends = steps + has_tail.astype(jnp.int32)
    for back in range(2, 0, -1):

        @pl.when(ends >= back)
        def _():
            step = ends - back
            for u in range(GROUP):

                @pl.when(step * GROUP + u < total)
                def _():
                    stage_copy(step % 2, u, 0).wait()

    each_zero(lambda copy: copy.wait())


def per_device(
    latent,
    destination,
    valid_frames,
    cache_slot,
    latent_cache,
    feature_cache,
    in_weight,
    in_bias,
    norm_gain,
    time_weight,
    time_bias,
    out_weight,
    out_bias,
):
    groups = lax.axis_size("req")
    tiles = lax.axis_size("tile")
    target = destination[:, 0]
    smem = pl.BlockSpec(memory_space=pltpu.SMEM)
    vmem = pl.BlockSpec(memory_space=pltpu.VMEM)
    hbm = pl.BlockSpec(memory_space=pltpu.HBM)
    shape = jax.ShapeDtypeStruct
    dma = pltpu.SemaphoreType.DMA
    slots = 8

    in_hbm = functools.partial(pltpu.with_memory_space_constraint, memory_space=pltpu.HBM)

    cached, patches, phase_weight = pl.pallas_call(
        functools.partial(exchange_kernel, groups, tiles),
        out_shape=(
            pltpu.VMEM((slots, 2, WINDOW, MIDDLE_CHANNELS), BF16),
            pltpu.VMEM((slots * SEQ * PATCH, WINDOW), BF16),
            pltpu.VMEM((6, OUTPUT_CHANNELS, 2 * MIDDLE_CHANNELS), BF16),
        ),
        in_specs=[hbm] * 7,
        out_specs=(vmem, vmem, vmem),
        scratch_shapes=[
            pltpu.SMEM((16,), jnp.int32),
            pltpu.SMEM((16,), jnp.int32),
            pltpu.SMEM((16,), jnp.int32),
            pltpu.VMEM((4, FRAMES, ROWS, LATENT_CHANNELS, WIDTH), BF16),
            pltpu.VMEM((16, 2, ROWS, LATENT_CHANNELS, WIDTH), BF16),
            pltpu.VMEM((16, 2, ROWS, WIDTH, MIDDLE_CHANNELS), BF16),
            pltpu.VMEM((3, 3, OUTPUT_CHANNELS, MIDDLE_CHANNELS), BF16),
            pltpu.VMEM((24, LATENT_CHANNELS, 128), BF16),
            pltpu.VMEM((2, slots, 2, WIDTH, MIDDLE_CHANNELS), BF16),
            pltpu.VMEM((3, 24, LATENT_CHANNELS, 128), BF16),
            pltpu.VMEM((3, 16, LATENT_CHANNELS, 128), BF16),
            pltpu.SMEM((slots,), jnp.int32),
            dma((3,)),
            dma((3,)),
            dma((4,)),
            dma((4,)),
            dma((2,)),
            dma((2,)),
            dma((7,)),
        ],
        compiler_params=pltpu.CompilerParams(
            collective_id=0, has_side_effects=True, vmem_limit_bytes=VMEM_LIMIT
        ),
        name="exchange",
    )(
        in_hbm(target),
        in_hbm(valid_frames),
        in_hbm(cache_slot),
        in_hbm(jnp.transpose(latent, (0, 1, 2, 4, 3))),
        in_hbm(jnp.transpose(latent_cache, (0, 1, 2, 4, 3))),
        in_hbm(feature_cache),
        in_hbm(jnp.transpose(out_weight, (0, 1, 3, 2))),
    )

    return pl.pallas_call(
        decode_kernel,
        out_shape=shape((slots, 2 * FRAMES, 2 * ROWS, 2 * WIDTH, OUTPUT_CHANNELS), BF16),
        in_specs=[smem, smem] + [vmem] * 9,
        out_specs=hbm,
        scratch_shapes=[
            pltpu.SMEM((slots,), jnp.int32),
            pltpu.SMEM((slots * FRAMES + 2 * GROUP,), jnp.int32),
            pltpu.VMEM((slots, SEQ, WINDOW, MIDDLE_CHANNELS), BF16),
            pltpu.VMEM((3, 2 * GROUP, WINDOW, MIDDLE_CHANNELS), BF16),
            pltpu.VMEM((2 * GROUP, 2 * ROWS, 2 * WIDTH, 128), F32),
            pltpu.VMEM((2 * GROUP, 2 * ROWS, 2 * WIDTH, 128), F32),
            pltpu.VMEM((2, GROUP, 2, 2 * ROWS, 2 * WIDTH, OUTPUT_CHANNELS), BF16),
            pltpu.VMEM((2 * FRAMES, 2 * ROWS, 2 * WIDTH, OUTPUT_CHANNELS), BF16),
            dma((slots, 3)),
            dma((2, GROUP)),
        ],
        compiler_params=pltpu.CompilerParams(vmem_limit_bytes=VMEM_LIMIT),
        name="decode",
    )(
        target,
        valid_frames,
        cached,
        patches,
        in_weight.reshape(27 * LATENT_CHANNELS, MIDDLE_CHANNELS),
        in_bias,
        norm_gain,
        time_weight.reshape(3 * MIDDLE_CHANNELS, 2 * MIDDLE_CHANNELS),
        time_bias,
        phase_weight,
        out_bias,
    )


def solution(mesh):
    placed = (
        P("req", None, "tile", None, None),
        P(),
        P(),
        P(),
        P("req", None, "tile", None, None),
        P("req", None, "tile", None, None),
        P(),
        P(),
        P(),
        P(),
        P(),
        P(),
        P(),
    )
    return jax.shard_map(
        per_device,
        mesh=mesh,
        in_specs=placed,
        out_specs=P("req", None, "tile", None, None),
        check_vma=False,
    )
```

```python
import functools

import jax
import jax.numpy as jnp
from jax import lax
from jax.experimental import pallas as pl
from jax.experimental.pallas import tpu as pltpu
from jax.sharding import PartitionSpec as P

LATENT_CHANNELS = 16
MIDDLE_CHANNELS = 384
OUTPUT_CHANNELS = 192
FRAMES = 4
CAPACITY = 2
EPSILON = 1e-06

ROWS = 2
WIDTH = 32
WINDOW = (ROWS + 2) * WIDTH
PATCH = 9 * LATENT_CHANNELS
SEQ = FRAMES + 2
GROUP = 4
VMEM_LIMIT = 28 * 2**20

MESH = pl.DeviceIdType.MESH
BF16 = jnp.bfloat16
F32 = jnp.float32


def pick_two(dest_ref, start, target):
    seen = jnp.int32(0)
    first = jnp.int32(0)
    second = jnp.int32(0)
    for j in range(4):
        hit = dest_ref[start + j] == target
        first = jnp.where(hit & (seen == 0), j, first)
        second = jnp.where(hit & (seen == 1), j, second)
        seen = seen + hit.astype(jnp.int32)
    return first, second, seen


def lane_join(pieces):
    return jnp.concatenate([p.astype(F32) for p in pieces], axis=-1).astype(BF16)


def exchange_kernel(
    groups,
    tiles,
    dest_hbm,
    valid_hbm,
    cache_slot_hbm,
    latent_hbm,
    latent_cache_hbm,
    feature_hbm,
    out_weight_hbm,
    cached_ref,
    patch_ref,
    phase_ref,
    dest_ref,
    valid_ref,
    cache_slot_ref,
    latent_ref,
    latent_cache_ref,
    feature_ref,
    out_weight_ref,
    packed_ref,
    feature_send,
    near_ref,
    far_send,
    far_ref,
    count_ref,
    near_ssem,
    near_rsem,
    far_ssem,
    far_rsem,
    feature_ssem,
    feature_rsem,
    load_sem,
):
    group = lax.axis_index("req")
    tile = lax.axis_index("tile")
    loads = [
        pltpu.make_async_copy(source, target, load_sem.at[i])
        for i, (source, target) in enumerate(
            (
                (dest_hbm, dest_ref),
                (cache_slot_hbm, cache_slot_ref),
                (valid_hbm, valid_ref),
                (latent_hbm, latent_ref),
                (latent_cache_hbm, latent_cache_ref),
                (feature_hbm, feature_ref),
                (out_weight_hbm, out_weight_ref),
            )
        )
    ]

    def peer(offset, turn):
        return (lax.rem(group + turn, groups), lax.rem(tile + offset + tiles, tiles))

    present = {-1: tile > 0, 0: None, 1: tile < tiles - 1}

    def where_present(offset, act):
        def run():
            act()

        if offset == 0:
            run()
        else:
            pl.when(present[offset])(run)

    barrier = pltpu.get_barrier_semaphore()
    for offset in (1, -1):
        where_present(
            offset,
            lambda: pl.semaphore_signal(
                barrier, inc=1, device_id=peer(offset, 0), device_id_type=MESH
            ),
        )
    for turn in range(1, 4):
        pl.semaphore_signal(barrier, inc=1, device_id=peer(0, turn), device_id_type=MESH)
    for load in loads:
        load.start()

    for load in loads[:3]:
        load.wait()

    cache_rows = []
    for source in range(4):
        first, second, seen = pick_two(dest_ref, 4 * source, group)
        for k, local in ((0, first), (1, second)):
            r = 4 * source + local
            cache_rows.append(cache_slot_ref[r])
            count_ref[2 * source + k] = jnp.where(seen > k, valid_ref[r], 0)
    picks = [
        pick_two(dest_ref, 4 * group, lax.rem(group + turn, groups))[:2] for turn in range(4)
    ]

    loads[3].wait()
    for local in range(4):
        for pair in range(2):
            block = lane_join(
                [latent_ref[local, 2 * pair + f, y] for f in range(2) for y in range(2)]
            )
            packed_ref[2 * local + pair] = block
            near_ref[1, 2 * local + pair] = block
    loads[4].wait()
    for slot in range(8):
        block = lane_join(
            [latent_cache_ref[cache_rows[slot], f, y] for f in range(2) for y in range(2)]
        )
        packed_ref[8 + slot] = block
        near_ref[1, 8 + slot] = block

    sides = (tile > 0).astype(jnp.int32) + (tile < tiles - 1).astype(jnp.int32)
    pl.semaphore_wait(barrier, 3 + sides)
    near = {
        offset: pltpu.make_async_remote_copy(
            src_ref=packed_ref,
            dst_ref=near_ref.at[1 - offset],
            send_sem=near_ssem.at[1 - offset],
            recv_sem=near_rsem.at[1 - offset],
            device_id=peer(offset, 0),
            device_id_type=MESH,
        )
        for offset in (1, -1)
    }
    for offset in (1, -1):
        where_present(offset, lambda: near[offset].start())

    loads[5].wait()
    for slot in range(8):
        for f in range(2):
            for edge in range(2):
                feature_send[edge, slot, f] = feature_ref[cache_rows[slot], f, edge]
    edges = {
        offset: pltpu.make_async_remote_copy(
            src_ref=feature_send.at[edge],
            dst_ref=cached_ref.at[:, :, at : at + WIDTH, :],
            send_sem=feature_ssem.at[edge],
            recv_sem=feature_rsem.at[edge],
            device_id=peer(offset, 0),
            device_id_type=MESH,
        )
        for edge, offset, at in ((1, 1, 0), (0, -1, WINDOW - WIDTH))
    }
    for offset in (1, -1):
        where_present(offset, lambda: edges[offset].start())
    for slot in range(8):
        for f in range(2):
            for y in range(ROWS):
                at = (1 + y) * WIDTH
                cached_ref[slot, f, at : at + WIDTH, :] = feature_send[y, slot, f]
    for place, gone in ((0, tile == 0), (2, tile == tiles - 1)):

        @pl.when(gone)
        def _():
            near_ref[place] = jnp.zeros((16, LATENT_CHANNELS, 128), BF16)

    for offset in (1, -1):
        where_present(-offset, lambda: near[offset].wait_recv())
    def route(turn, target_ref):
        for place in range(3):
            for k in range(CAPACITY):
                for pair in range(2):
                    target_ref[turn, place, 2 * k + pair] = near_ref[
                        place, 2 * picks[turn][k] + pair
                    ]

    far = []
    for turn in (2, 1, 3):
        route(turn, far_send)
        far.append(
            pltpu.make_async_remote_copy(
                src_ref=far_send.at[turn],
                dst_ref=far_ref.at[turn],
                send_sem=far_ssem.at[turn],
                recv_sem=far_rsem.at[turn],
                device_id=peer(0, turn),
                device_id_type=MESH,
            )
        )
        far[-1].start()
    route(0, far_ref)
    loads[6].wait()

    def combine(i, carry):
        at = pl.multiple_of(i * 16, 16)
        taps = [
            [out_weight_ref[b, c, pl.ds(at, 16), :].astype(F32) for c in range(3)] for b in range(3)
        ]
        rows = (
            (taps[0], [u + v for u, v in zip(taps[1], taps[2])]),
            ([u + v for u, v in zip(taps[0], taps[1])], taps[2]),
        )
        for py in range(2):
            for ty in range(2):
                left, middle, right = rows[py][ty]
                k = ty * MIDDLE_CHANNELS
                for part, value in enumerate((left, left + middle + right, right)):
                    phase_ref[3 * py + part, pl.ds(at, 16), k : k + MIDDLE_CHANNELS] = value.astype(
                        BF16
                    )
        return carry

    lax.fori_loop(0, OUTPUT_CHANNELS // 16, combine, 0)
    for copy in far:
        copy.wait_recv()

    lane = lax.broadcasted_iota(jnp.int32, (LATENT_CHANNELS, 128), 1)
    column = lane % WIDTH

    def turned(value, by):
        return pltpu.roll(value, by % 128, 1)

    def gather_patches(slot, carry):
        count = count_ref[slot]
        turn = lax.rem(group - slot // 2 + 4, 4)
        k = slot % 2
        for pair in range(3):
            blocks = []
            for place in range(3):
                if pair == 0:
                    block = near_ref[place, 8 + slot].astype(F32)
                else:
                    block = far_ref[turn, place, 2 * k + pair - 1].astype(F32)
                    frame = 2 * (pair - 1) + lane // 64
                    block = jnp.where(frame < count, block, 0.0)
                if place == 0:
                    block = jnp.where(tile > 0, block, 0.0)
                if place == 2:
                    block = jnp.where(tile < tiles - 1, block, 0.0)
                blocks.append(block)
            up, own, down = blocks
            own_half = turned(own, 64)
            windows = (
                (
                    jnp.where(lane < 64, up, own_half),
                    jnp.where(
                        lane < 32,
                        turned(up, -32),
                        jnp.where(lane < 96, turned(own, 32), turned(down, -32)),
                    ),
                    jnp.where(lane < 64, own, turned(down, 64)),
                ),
                (
                    jnp.where(lane < 64, turned(up, 64), own),
                    jnp.where(
                        lane < 32,
                        turned(up, 32),
                        jnp.where(lane < 96, turned(own, -32), turned(down, 32)),
                    ),
                    jnp.where(lane < 64, own_half, down),
                ),
            )
            for half in range(2):
                base = (slot * SEQ + 2 * pair + half) * PATCH
                for b in range(3):
                    window = windows[half][b]
                    shifted = (
                        jnp.where(column == 0, 0.0, turned(window, 1)),
                        window,
                        jnp.where(column == WIDTH - 1, 0.0, turned(window, -1)),
                    )
                    for c in range(3):
                        at = pl.multiple_of(base + (3 * b + c) * 16, 16)
                        patch_ref[pl.ds(at, 16), :] = shifted[c].astype(BF16)
        return carry

    lax.fori_loop(0, 8, gather_patches, 0, unroll=2)
    for copy in far:
        copy.wait_send()
    for offset in (1, -1):
        where_present(offset, lambda: near[offset].wait_send())
        where_present(offset, lambda: edges[offset].wait_send())
        where_present(-offset, lambda: edges[offset].wait_recv())

    for edge, gone in ((0, tile == 0), (WINDOW - WIDTH, tile == tiles - 1)):

        @pl.when(gone)
        def _():
            cached_ref[:, :, edge : edge + WIDTH, :] = jnp.zeros(
                (8, 2, WIDTH, MIDDLE_CHANNELS), BF16
            )


def decode_kernel(
    dest_ref,
    valid_ref,
    cached_ref,
    patch_ref,
    in_weight_ref,
    in_bias_ref,
    gain_ref,
    time_weight_ref,
    time_bias_ref,
    out_weight_ref,
    out_bias_ref,
    out_ref,
    count_ref,
    work_ref,
    seq_ref,
    shift_ref,
    low_ref,
    high_ref,
    stage_ref,
    zero_ref,
    zero_sem,
    stage_sem,
):
    group = lax.axis_index("req")
    tile = lax.axis_index("tile")
    tiles = lax.axis_size("tile")

    total = jnp.int32(0)
    last = jnp.int32(0)
    for source in range(4):
        first, second, seen = pick_two(dest_ref, 4 * source, group)
        for k, local in ((0, first), (1, second)):
            slot = 2 * source + k
            count = jnp.where(seen > k, valid_ref[4 * source + local], 0)
            count_ref[slot] = count
            for f in range(FRAMES):
                work_ref[total] = jnp.int32(slot * FRAMES + f)
                keep = f < count
                last = jnp.where(keep, slot * FRAMES + f, last)
                total = total + keep.astype(jnp.int32)
    for extra in range(2 * GROUP):
        work_ref[total + extra] = last
    steps = (total + 1) // GROUP
    has_tail = total > steps * GROUP

    zero_ref[...] = jnp.zeros_like(zero_ref)

    def each_zero(act):
        @pl.loop(0, 8)
        def _(slot):
            count = count_ref[slot]
            missing = FRAMES - count
            for size in (1, 2, 4):
                at = 2 * jnp.where(size == 1, count, FRAMES - size)

                @pl.when((missing & size) > 0)
                def _():
                    act(
                        pltpu.make_async_copy(
                            zero_ref.at[pl.ds(0, 2 * size)],
                            out_ref.at[slot, pl.ds(at, 2 * size)],
                            zero_sem.at[slot, size // 2],
                        )
                    )

    each_zero(lambda copy: copy.start())

    for slot in range(8):

        @pl.when(count_ref[slot] > 0)
        def _():
            seq_ref[slot, 0:2] = cached_ref[slot]

    half_gain = 0.5 * gain_ref[...][None, :]
    in_bias = in_bias_ref[...][None, :]

    def in_conv(step):
        for part in range(GROUP // 2):
            places = []
            pieces = []
            for u in range(2):
                item = work_ref[step * GROUP + 2 * part + u]
                slot, f = item // FRAMES, item % FRAMES
                places.append((slot, f))
                at = pl.multiple_of((slot * SEQ + f) * PATCH, 16)
                pieces.append(patch_ref[pl.ds(at, 3 * PATCH), :])
            inner = (
                lax.dot_general(
                    jnp.concatenate(pieces, axis=1),
                    in_weight_ref[...],
                    (((0,), (0,)), ((), ())),
                    preferred_element_type=F32,
                )
                + in_bias
            )
            scale = lax.rsqrt(jnp.mean(inner * inner, axis=-1, keepdims=True) + EPSILON)
            half = inner * scale * half_gain
            active = (half + half * jnp.tanh(half)).astype(BF16)
            for u, (slot, f) in enumerate(places):
                seq_ref[slot, f + 2] = active[u * WINDOW : (u + 1) * WINDOW]

    pixel_column = lax.broadcasted_iota(jnp.int32, (WINDOW, 2 * MIDDLE_CHANNELS), 0) % WIDTH
    first_column = pixel_column == 0
    last_column = pixel_column == WIDTH - 1

    def stage_copy(buffer, u, item):
        return pltpu.make_async_copy(
            stage_ref.at[buffer, u],
            out_ref.at[item // FRAMES, pl.ds(2 * (item % FRAMES), 2)],
            stage_sem.at[buffer, u],
        )

    @pl.when(total > 0)
    def _():
        in_conv(0)

    def decode_items(step, size):
        buffer = step % 2
        items = [work_ref[step * GROUP + u] for u in range(size)]
        rows = []
        for u in range(size):
            slot, f = items[u] // FRAMES, items[u] % FRAMES
            rows.append(jnp.concatenate([seq_ref[slot, f + a] for a in range(3)], axis=1))
        doubled = (
            jnp.dot(
                jnp.concatenate(rows, axis=0), time_weight_ref[...], preferred_element_type=F32
            )
            + time_bias_ref[...][None, :]
        )
        for u in range(size):
            own = doubled[u * WINDOW : (u + 1) * WINDOW]
            own = jnp.concatenate(
                [
                    jnp.where(tile > 0, own[:WIDTH], 0.0),
                    own[WIDTH : WINDOW - WIDTH],
                    jnp.where(tile < tiles - 1, own[WINDOW - WIDTH :], 0.0),
                ],
                axis=0,
            )
            middle = own.astype(BF16)
            before = jnp.where(first_column, 0.0, pltpu.roll(own, 1, 0).astype(BF16))
            after = jnp.where(last_column, 0.0, pltpu.roll(own, WINDOW - 1, 0).astype(BF16))
            for c, value in enumerate((before - middle, middle, after - middle)):
                for h in range(2):
                    shift_ref[c, 2 * u + h] = value[:, h * MIDDLE_CHANNELS : (h + 1) * MIDDLE_CHANNELS]

        if size == GROUP:
            in_conv(step + 1)
        for py in range(2):
            products = []
            for part in range(3):
                taps = []
                for ty in range(2):
                    a = (py + ty) * WIDTH
                    taps.append(
                        shift_ref[part, 0 : 2 * size, a : a + ROWS * WIDTH, :].reshape(
                            2 * size * ROWS * WIDTH, MIDDLE_CHANNELS
                        )
                    )
                products.append(
                    lax.dot_general(
                        jnp.concatenate(taps, axis=1),
                        out_weight_ref[3 * py + part],
                        (((1,), (1,)), ((), ())),
                        preferred_element_type=F32,
                    )
                )
            shared = products[1] + out_bias_ref[...][None, :]
            for px in range(2):
                result = shared + products[2 * px]
                for q in range(2 * size):
                    for y in range(ROWS):
                        at = (q * ROWS + y) * WIDTH
                        spread = pl.ds(px, WIDTH, stride=2)
                        part = result[at : at + WIDTH]
                        low_ref[q, 2 * y + py, spread, :] = part[:, :128]
                        high_ref[q, 2 * y + py, spread, 0 : OUTPUT_CHANNELS - 128] = part[:, 128:]

        @pl.when(step >= 2)
        def _():
            for u in range(GROUP):
                stage_copy(buffer, u, 0).wait()

        for u in range(size):
            stage_ref[buffer, u, :, :, :, 0:128] = low_ref[2 * u : 2 * u + 2].astype(BF16)
            stage_ref[buffer, u, :, :, :, 128:OUTPUT_CHANNELS] = high_ref[
                2 * u : 2 * u + 2, :, :, 0 : OUTPUT_CHANNELS - 128
            ].astype(BF16)
            if u == 0:
                stage_copy(buffer, u, items[u]).start()
            else:

                @pl.when(step * GROUP + u < total)
                def _():
                    stage_copy(buffer, u, items[u]).start()

    @pl.loop(0, steps)
    def _(step):
        decode_items(step, GROUP)

    @pl.when(has_tail)
    def _():
        decode_items(steps, GROUP // 2)

    ends = steps + has_tail.astype(jnp.int32)
    for back in range(2, 0, -1):

        @pl.when(ends >= back)
        def _():
            step = ends - back
            for u in range(GROUP):

                @pl.when(step * GROUP + u < total)
                def _():
                    stage_copy(step % 2, u, 0).wait()

    each_zero(lambda copy: copy.wait())


def per_device(
    latent,
    destination,
    valid_frames,
    cache_slot,
    latent_cache,
    feature_cache,
    in_weight,
    in_bias,
    norm_gain,
    time_weight,
    time_bias,
    out_weight,
    out_bias,
):
    groups = lax.axis_size("req")
    tiles = lax.axis_size("tile")
    target = destination[:, 0]
    smem = pl.BlockSpec(memory_space=pltpu.SMEM)
    vmem = pl.BlockSpec(memory_space=pltpu.VMEM)
    hbm = pl.BlockSpec(memory_space=pltpu.HBM)
    shape = jax.ShapeDtypeStruct
    dma = pltpu.SemaphoreType.DMA
    slots = 8

    in_hbm = functools.partial(pltpu.with_memory_space_constraint, memory_space=pltpu.HBM)

    cached, patches, phase_weight = pl.pallas_call(
        functools.partial(exchange_kernel, groups, tiles),
        out_shape=(
            pltpu.VMEM((slots, 2, WINDOW, MIDDLE_CHANNELS), BF16),
            pltpu.VMEM((slots * SEQ * PATCH, WINDOW), BF16),
            pltpu.VMEM((6, OUTPUT_CHANNELS, 2 * MIDDLE_CHANNELS), BF16),
        ),
        in_specs=[hbm] * 7,
        out_specs=(vmem, vmem, vmem),
        scratch_shapes=[
            pltpu.SMEM((16,), jnp.int32),
            pltpu.SMEM((16,), jnp.int32),
            pltpu.SMEM((16,), jnp.int32),
            pltpu.VMEM((4, FRAMES, ROWS, LATENT_CHANNELS, WIDTH), BF16),
            pltpu.VMEM((16, 2, ROWS, LATENT_CHANNELS, WIDTH), BF16),
            pltpu.VMEM((16, 2, ROWS, WIDTH, MIDDLE_CHANNELS), BF16),
            pltpu.VMEM((3, 3, OUTPUT_CHANNELS, MIDDLE_CHANNELS), BF16),
            pltpu.VMEM((16, LATENT_CHANNELS, 128), BF16),
            pltpu.VMEM((2, slots, 2, WIDTH, MIDDLE_CHANNELS), BF16),
            pltpu.VMEM((3, 16, LATENT_CHANNELS, 128), BF16),
            pltpu.VMEM((4, 3, 4, LATENT_CHANNELS, 128), BF16),
            pltpu.VMEM((4, 3, 4, LATENT_CHANNELS, 128), BF16),
            pltpu.SMEM((slots,), jnp.int32),
            dma((3,)),
            dma((3,)),
            dma((4,)),
            dma((4,)),
            dma((2,)),
            dma((2,)),
            dma((7,)),
        ],
        compiler_params=pltpu.CompilerParams(
            collective_id=0, has_side_effects=True, vmem_limit_bytes=VMEM_LIMIT
        ),
        name="exchange",
    )(
        in_hbm(target),
        in_hbm(valid_frames),
        in_hbm(cache_slot),
        in_hbm(jnp.transpose(latent, (0, 1, 2, 4, 3))),
        in_hbm(jnp.transpose(latent_cache, (0, 1, 2, 4, 3))),
        in_hbm(feature_cache),
        in_hbm(jnp.transpose(out_weight, (0, 1, 3, 2))),
    )

    return pl.pallas_call(
        decode_kernel,
        out_shape=shape((slots, 2 * FRAMES, 2 * ROWS, 2 * WIDTH, OUTPUT_CHANNELS), BF16),
        in_specs=[smem, smem] + [vmem] * 9,
        out_specs=hbm,
        scratch_shapes=[
            pltpu.SMEM((slots,), jnp.int32),
            pltpu.SMEM((slots * FRAMES + 2 * GROUP,), jnp.int32),
            pltpu.VMEM((slots, SEQ, WINDOW, MIDDLE_CHANNELS), BF16),
            pltpu.VMEM((3, 2 * GROUP, WINDOW, MIDDLE_CHANNELS), BF16),
            pltpu.VMEM((2 * GROUP, 2 * ROWS, 2 * WIDTH, 128), F32),
            pltpu.VMEM((2 * GROUP, 2 * ROWS, 2 * WIDTH, 128), F32),
            pltpu.VMEM((2, GROUP, 2, 2 * ROWS, 2 * WIDTH, OUTPUT_CHANNELS), BF16),
            pltpu.VMEM((2 * FRAMES, 2 * ROWS, 2 * WIDTH, OUTPUT_CHANNELS), BF16),
            dma((slots, 3)),
            dma((2, GROUP)),
        ],
        compiler_params=pltpu.CompilerParams(vmem_limit_bytes=VMEM_LIMIT),
        name="decode",
    )(
        target,
        valid_frames,
        cached,
        patches,
        in_weight.reshape(27 * LATENT_CHANNELS, MIDDLE_CHANNELS),
        in_bias,
        norm_gain,
        time_weight.reshape(3 * MIDDLE_CHANNELS, 2 * MIDDLE_CHANNELS),
        time_bias,
        phase_weight,
        out_bias,
    )


def solution(mesh):
    placed = (
        P("req", None, "tile", None, None),
        P(),
        P(),
        P(),
        P("req", None, "tile", None, None),
        P("req", None, "tile", None, None),
        P(),
        P(),
        P(),
        P(),
        P(),
        P(),
        P(),
    )
    return jax.shard_map(
        per_device,
        mesh=mesh,
        in_specs=placed,
        out_specs=P("req", None, "tile", None, None),
        check_vma=False,
    )
```
